32 devices in a mesh: seq: 16 (over z, y, core), tp: 2 (over x).
Axes of the slice: x: 2, y: 2, z: 4, core: 2. Of those that a mesh axis runs over, the one named last changes fastest.
Arguments:
- tokens: bfloat16 [8192, 2880], P(('seq', 'tp')), may hold values from -24 to 24
- w_query: bfloat16 [2880, 4096], P('seq', 'tp')
- w_kv: bfloat16 [2880, 1024], P('seq', 'tp')
- w_out: bfloat16 [2880, 4096], P('seq', 'tp'), may hold values from -0.5 to 0.5
- sinks: float32 [64], P('tp'), may hold values from 1 to 6
Outputs:
- attn_out: bfloat16 [8192, 2880], P(('seq', 'tp'))
The draws below stay inside these ranges and needn't reach their ends.
All inputs are finite; a program needn't handle non-finite values.
Results may differ from the reference program's by a relative error of at most 0.015.
Values may be sent and summed in bfloat16 or wider, within the bound.
No kernel may reach another device: no remote copies, remote signals or barrier semaphores. Data moves between devices by JAX's collectives and lax.ppermute only.
A program may use at most 128 MiB of HBM per device.

```python
import math
import jax
import jax.numpy as jnp
from jax import lax

MODEL_WIDTH = 2880
QUERY_HEADS = 64
KEY_VALUE_HEADS = 8
HEAD_WIDTH = 64
WINDOW_KEYS = 128
TOKENS = 8192
N_TP = 2


def query_weight_matrix(key):
    base_key = jax.random.fold_in(key, 101)
    sample_input = jnp.clip(jax.random.normal(base_key, (MODEL_WIDTH, QUERY_HEADS * HEAD_WIDTH), jnp.float32), -4.0, 4.0)
    return sample_input * MODEL_WIDTH ** (-0.5)


def draw_w_query(key, part):
    return query_weight_matrix(key).astype(jnp.bfloat16)


def draw_w_kv(key, part):
    sample_input = jnp.clip(jax.random.normal(jax.random.fold_in(key, 202), (MODEL_WIDTH, KEY_VALUE_HEADS, 2, HEAD_WIDTH), jnp.float32), -4.0, 4.0) * MODEL_WIDTH ** (-0.5)
    return sample_input.reshape(MODEL_WIDTH, KEY_VALUE_HEADS * 2 * HEAD_WIDTH).astype(jnp.bfloat16)


def draw_tokens(key, part):
    sample_input = jnp.clip(jax.random.normal(jax.random.fold_in(key, 303), (TOKENS, MODEL_WIDTH), jnp.float32), -6.0, 6.0)
    return sample_input.astype(jnp.bfloat16)


def block_levels(key, extent, split, smallest, largest):
    loudness = 1.0
    for dim, shards_of in split:
        draws = jax.random.uniform(jax.random.fold_in(jax.random.fold_in(key, 6), dim), (shards_of,), jnp.float32, smallest / len(split), largest / len(split))
        loudness = loudness * jnp.repeat(jnp.exp(draws), extent[dim] // shards_of).reshape((-1,) + (1,) * (len(extent) - 1 - dim))
    return loudness


def bell_draw(stream_key, dims, spread, limit, split=(), kind=jnp.bfloat16):
    values = jax.random.normal(stream_key, dims, jnp.float32) * spread
    if len(split) > 0:
        values = block_levels(stream_key, dims, split, -0.22, 0.18) * values
    return jnp.clip(values, min=-limit, max=limit).astype(kind)


def setup_inputs(seed: int = 0) -> dict:
    splits = jax.random.split(jax.random.key(seed), 6)
    tokens = draw_tokens(jax.random.fold_in(splits[5], 71), 0)
    w_query = draw_w_query(jax.random.fold_in(splits[5], 71), 0)
    w_kv = draw_w_kv(jax.random.fold_in(splits[5], 71), 0)
    w_out = bell_draw(splits[3], (MODEL_WIDTH, QUERY_HEADS * HEAD_WIDTH), (QUERY_HEADS * HEAD_WIDTH * 4 // WINDOW_KEYS) ** -0.5, 0.5, ((0, 16), (1, 2)))
    sinks = jnp.clip(1.0 + 5.0 * jax.random.uniform(splits[4], (QUERY_HEADS,), jnp.float32) ** block_levels(splits[4], (QUERY_HEADS,), ((0, 2),), -0.2, 0.2), 1.0, 6.0)
    return dict(tokens=tokens, w_query=w_query, w_kv=w_kv, w_out=w_out, sinks=sinks)


rope_base = 150000.0


def rotary(vectors, places):
    half_dim = vectors.shape[-1] // 2
    frequency = jnp.exp(jnp.arange(half_dim, dtype=jnp.float32) * (-2.0 * math.log(rope_base) / vectors.shape[-1]))
    angles = places.astype(jnp.float32)[:, None, None] * frequency[None, None, :]
    cosine = jnp.cos(angles)
    sine = jnp.sin(angles)
    lower_half = vectors[..., :half_dim]
    upper_half = vectors[..., half_dim:]
    return jnp.concatenate([lower_half * cosine - upper_half * sine, upper_half * cosine + lower_half * sine], axis=-1)


def attend(query_rows, key_value_rows, sink_scores, query_pos, key_pos):
    key_part = key_value_rows[:, :, 0, :].astype(jnp.float32)
    value_part = key_value_rows[:, :, 1, :].astype(jnp.float32)
    scores = jnp.einsum("qhgd,khd->hgqk", query_rows.astype(jnp.float32), key_part) * (HEAD_WIDTH ** -0.5)
    allowed = (key_pos[None, :] <= query_pos[:, None]) & (key_pos[None, :] > query_pos[:, None] - WINDOW_KEYS) & (key_pos[None, :] >= 0)
    scores = jnp.where(allowed[None, None], scores, -jnp.inf)
    row_max = jnp.maximum(jnp.max(scores, axis=-1), sink_scores[:, :, None])
    exponent = jnp.exp(scores - row_max[..., None])
    denominator = jnp.sum(exponent, axis=-1) + jnp.exp(sink_scores[:, :, None] - row_max)
    weights = exponent.astype(jnp.bfloat16)
    mixture = jnp.einsum("hgqk,khd->qhgd", weights.astype(jnp.float32), value_part)
    return (mixture / jnp.transpose(denominator, (2, 0, 1))[..., None]).astype(jnp.bfloat16)


def reference(tokens, w_query, w_kv, w_out, sinks):
    total_row_count = tokens.shape[0]
    head_groups = QUERY_HEADS // KEY_VALUE_HEADS
    query_full = jnp.dot(tokens, w_query, preferred_element_type=jnp.float32)
    key_value_full = jnp.dot(tokens, w_kv, preferred_element_type=jnp.float32)
    places = jnp.arange(total_row_count, dtype=jnp.int32)
    query_rows = rotary(query_full.reshape(total_row_count, QUERY_HEADS, HEAD_WIDTH), places).astype(jnp.bfloat16)
    query_rows = query_rows.reshape(total_row_count, KEY_VALUE_HEADS, head_groups, HEAD_WIDTH)
    split_key_value = key_value_full.reshape(total_row_count, KEY_VALUE_HEADS, 2, HEAD_WIDTH)
    key_value_rows = jnp.stack([rotary(split_key_value[:, :, 0, :], places), split_key_value[:, :, 1, :]], axis=2).astype(jnp.bfloat16)
    padded_rows = jnp.concatenate([jnp.zeros((WINDOW_KEYS, KEY_VALUE_HEADS, 2, HEAD_WIDTH), jnp.bfloat16), key_value_rows], axis=0)
    block_rows = math.gcd(total_row_count, 512)
    sink_scores = sinks.reshape(KEY_VALUE_HEADS, head_groups)

    def one_block(block_index):
        first_row = (block_index * block_rows).astype(jnp.int32)
        q_block = lax.dynamic_slice_in_dim(query_rows, first_row, block_rows, 0)
        kv_block = lax.dynamic_slice_in_dim(padded_rows, first_row, block_rows + WINDOW_KEYS, 0)
        query_pos = first_row + jnp.arange(block_rows, dtype=jnp.int32)
        key_pos = first_row - WINDOW_KEYS + jnp.arange(block_rows + WINDOW_KEYS, dtype=jnp.int32)
        return attend(q_block, kv_block, sink_scores, query_pos, key_pos)

    blocks = lax.map(one_block, jnp.arange(total_row_count // block_rows, dtype=jnp.int32))
    attended = blocks.reshape(total_row_count, QUERY_HEADS * HEAD_WIDTH)
    group_cols = QUERY_HEADS * HEAD_WIDTH // N_TP
    result = jnp.zeros((total_row_count, MODEL_WIDTH), jnp.float32)
    for group in range(N_TP):
        att_part = attended[:, group * group_cols:(group + 1) * group_cols]
        w_part = w_out[:, group * group_cols:(group + 1) * group_cols]
        partial_sum = lax.dot_general(att_part, w_part, (((1,), (1,)), ((), ())), preferred_element_type=jnp.float32)
        result = result + partial_sum.astype(jnp.bfloat16).astype(jnp.float32)
    return result.astype(jnp.bfloat16)
```

```python
import functools
import math

import jax
import jax.numpy as jnp
from jax import lax
from jax.experimental import pallas as pl
from jax.experimental.pallas import tpu as pltpu
from jax.sharding import PartitionSpec as P

HEAD_WIDTH = 64
WINDOW_KEYS = 128
SLICES = 4

rope_base = 150000.0
vmem_bytes = 48 * 1024 * 1024


def shift(value, axis, by):
    devices = lax.axis_size(axis)
    pairs = [(i, i + by) for i in range(devices) if 0 <= i + by < devices]
    return lax.ppermute(value, axis, pairs)


def angles_of(places):
    half_dim = HEAD_WIDTH // 2
    frequency = jnp.exp(
        jnp.arange(half_dim, dtype=jnp.float32) * (-2.0 * math.log(rope_base) / HEAD_WIDTH)
    )
    return places.astype(jnp.float32)[None, :] * frequency[:, None]


def project_kernel(zs, tok, w0, w1, w2, w3, cosine, sine, kv_out, q_out, *, depth):
    total = None
    for k, w in enumerate((w0, w1, w2, w3)):
        rows = pl.ds(pl.multiple_of(zs[k] * depth, 16), depth)
        term = lax.dot_general(
            w[...], tok[0, rows, :], (((1,), (0,)), ((), ())), preferred_element_type=jnp.float32
        )
        total = term if total is None else total + term
    cos, sin = cosine[...], sine[...]
    half = HEAD_WIDTH // 2

    def rotated(at):
        lower, upper = total[at : at + half], total[at + half : at + 2 * half]
        return jnp.concatenate([lower * cos - upper * sin, upper * cos + lower * sin], axis=0)

    kv_out[0:HEAD_WIDTH] = rotated(0).astype(jnp.bfloat16)
    kv_out[HEAD_WIDTH : 2 * HEAD_WIDTH] = total[HEAD_WIDTH : 2 * HEAD_WIDTH].astype(jnp.bfloat16)
    for h in range(q_out.shape[0] // HEAD_WIDTH):
        q_out[h * HEAD_WIDTH : (h + 1) * HEAD_WIDTH] = rotated((h + 2) * HEAD_WIDTH).astype(jnp.bfloat16)


def project(zs, tok, weights, cosine, sine):
    blocks, features, block = tok.shape
    width, depth = weights[0].shape
    kv_width = 2 * HEAD_WIDTH
    whole = pl.BlockSpec((width, depth), lambda j, zs: (0, 0))
    angle = pl.BlockSpec((HEAD_WIDTH // 2, block), lambda j, zs: (0, j))
    return pl.pallas_call(
        functools.partial(project_kernel, depth=depth),
        grid_spec=pltpu.PrefetchScalarGridSpec(
            num_scalar_prefetch=1,
            grid=(blocks,),
            in_specs=[pl.BlockSpec((1, features, block), lambda j, zs: (j, 0, 0))]
            + [whole] * 4
            + [angle, angle],
            out_specs=[
                pl.BlockSpec((kv_width, block), lambda j, zs: (0, j)),
                pl.BlockSpec((width - kv_width, block), lambda j, zs: (0, j)),
            ],
        ),
        out_shape=[
            jax.ShapeDtypeStruct((kv_width, blocks * block), jnp.bfloat16),
            jax.ShapeDtypeStruct((width - kv_width, blocks * block), jnp.bfloat16),
        ],
        compiler_params=pltpu.CompilerParams(vmem_limit_bytes=vmem_bytes),
        cost_estimate=pl.CostEstimate(
            flops=2 * width * features * blocks * block,
            bytes_accessed=2 * features * (blocks * block + width),
            transcendentals=0,
        ),
        name="project",
    )(zs, tok, *weights, cosine, sine)


def attend_kernel(first, sinks, q, kv_before, kv_own, out):
    window = WINDOW_KEYS
    keys = jnp.concatenate([kv_before[:HEAD_WIDTH], kv_own[:HEAD_WIDTH]], axis=1)
    values = jnp.concatenate([kv_before[HEAD_WIDTH:], kv_own[HEAD_WIDTH:]], axis=1)
    keys = jnp.transpose(keys)
    row = lax.broadcasted_iota(jnp.int32, (2 * window, window), 0)
    lane = lax.broadcasted_iota(jnp.int32, (2 * window, window), 1)
    start = jnp.where(first[0] + pl.program_id(0) == 0, window, 0)
    allowed = (row > lane) & (row <= lane + window) & (row >= start)
    bias = jnp.where(allowed, 0.0, -jnp.inf)
    bias = jnp.concatenate([bias, bias], axis=1)
    log2e = math.log2(math.e)
    heads = q.shape[0] // HEAD_WIDTH
    left = lax.broadcasted_iota(jnp.int32, (1, 2 * window), 1) < window
    for h in range(0, heads, 2):
        at = h * HEAD_WIDTH
        pair = jnp.concatenate([q[at : at + HEAD_WIDTH], q[at + HEAD_WIDTH : at + 2 * HEAD_WIDTH]], axis=1)
        scores = jnp.dot(keys, pair, preferred_element_type=jnp.float32)
        scores = scores * (HEAD_WIDTH**-0.5 * log2e) + bias
        sink = jnp.where(left, sinks[h], sinks[h + 1]) * log2e
        top = jnp.maximum(jnp.max(scores, axis=0, keepdims=True), sink)
        exponent = jnp.exp2(scores - top)
        denominator = jnp.sum(exponent, axis=0, keepdims=True) + jnp.exp2(sink - top)
        mixture = jnp.dot(values, exponent.astype(jnp.bfloat16), preferred_element_type=jnp.float32)
        result = (mixture * (1.0 / denominator)).astype(jnp.bfloat16)
        out[at : at + HEAD_WIDTH] = result[:, :window]
        out[at + HEAD_WIDTH : at + 2 * HEAD_WIDTH] = result[:, window:]


def attend(first, sinks, q, kv):
    width, tokens = q.shape
    window = WINDOW_KEYS
    kv_width = 2 * HEAD_WIDTH
    return pl.pallas_call(
        attend_kernel,
        grid_spec=pltpu.PrefetchScalarGridSpec(
            num_scalar_prefetch=2,
            grid=(tokens // window,),
            in_specs=[
                pl.BlockSpec((width, window), lambda i, *_: (0, i)),
                pl.BlockSpec((kv_width, window), lambda i, *_: (0, i)),
                pl.BlockSpec((kv_width, window), lambda i, *_: (0, i + 1)),
            ],
            out_specs=pl.BlockSpec((width, window), lambda i, *_: (0, i)),
        ),
        out_shape=jax.ShapeDtypeStruct((width, tokens), jnp.bfloat16),
        compiler_params=pltpu.CompilerParams(vmem_limit_bytes=vmem_bytes),
        cost_estimate=pl.CostEstimate(
            flops=8 * width * tokens * window, bytes_accessed=4 * width * tokens, transcendentals=0
        ),
        name="attend",
    )(first, sinks, q, kv, kv)


def output_kernel(order, w, attended, out):
    out[0] = jnp.dot(w[...], attended[...], preferred_element_type=jnp.float32).astype(jnp.bfloat16)


def output_terms(order, w, attended):
    depth, width = w.shape
    blocks = order.shape[0]
    block = attended.shape[1] // blocks
    return pl.pallas_call(
        output_kernel,
        grid_spec=pltpu.PrefetchScalarGridSpec(
            num_scalar_prefetch=1,
            grid=(blocks,),
            in_specs=[
                pl.BlockSpec((depth, width), lambda r, order: (0, 0)),
                pl.BlockSpec((width, block), lambda r, order: (0, order[r])),
            ],
            out_specs=pl.BlockSpec((1, depth, block), lambda r, order: (r, 0, 0)),
        ),
        out_shape=jax.ShapeDtypeStruct((blocks, depth, block), jnp.bfloat16),
        compiler_params=pltpu.CompilerParams(vmem_limit_bytes=vmem_bytes),
        cost_estimate=pl.CostEstimate(
            flops=2 * width * depth * blocks * block,
            bytes_accessed=2 * (depth * width + (depth + width) * blocks * block),
            transcendentals=0,
        ),
        name="output_terms",
    )(order, w, attended)


def slab_body(tokens, w_query, w_kv, w_out, sinks):
    devices = lax.axis_size("seq")
    slabs = devices // SLICES
    tp = lax.axis_size("tp")
    place = lax.axis_index("seq")
    slab, part = place // SLICES, place % SLICES
    side = lax.axis_index("tp")
    block = tokens.shape[0]
    blocks = SLICES * tp
    both = ("seq", "tp")

    def swap(value, flip_seq, flip_tp):
        pairs = [
            (s * tp + t, (s ^ flip_seq) * tp + (t ^ flip_tp)) for s in range(devices) for t in range(tp)
        ]
        return lax.ppermute(value, both, pairs)

    def turn(value):
        pairs = [(s, (s + SLICES) % devices) for s in range(devices)]
        return lax.ppermute(value, "seq", pairs)

    groups = [
        [s * tp + t for s in range(z * SLICES, (z + 1) * SLICES) for t in range(tp)] for z in range(slabs)
    ]
    slab_tokens = lax.all_gather(
        tokens.T, both, axis=0, tiled=False, axis_index_groups=groups
    )

    def of_head(weight, head):
        width = weight.shape[1] // SLICES
        return lax.dynamic_slice_in_dim(weight, head * width, width, 1)

    def of_slab(make):
        pieces = jnp.stack(
            [make(part)] + [swap(make(part ^ flip), flip, 0) for flip in range(1, SLICES)]
        )
        rows, width = pieces.shape[1:]
        pieces = pieces.reshape(2, 2, rows, width)
        pieces = jnp.where(part % 2 == 1, pieces[:, ::-1], pieces)
        pieces = jnp.where(part // 2 == 1, pieces[::-1], pieces)
        return pieces.reshape(SLICES * rows, width)

    def round_slabs(own):
        held = [own]
        for _ in range(slabs - 1):
            held.append(turn(held[-1]))
        return held

    own_in = of_slab(lambda head: jnp.concatenate([of_head(w_kv, head), of_head(w_query, head)], axis=1))
    own_out = of_slab(lambda head: of_head(w_out, head))
    weights_in = round_slabs(own_in)
    weights_out = round_slabs(own_out)

    first = slab * (blocks * block)
    places = first + jnp.arange(blocks * block, dtype=jnp.int32)
    angles = angles_of(places)
    slabs_held = (slab - jnp.arange(slabs, dtype=jnp.int32)) % slabs
    kv, q = project(slabs_held, slab_tokens, [w.T for w in weights_in], jnp.cos(angles), jnp.sin(angles))
    kv_tail = shift(kv[:, -WINDOW_KEYS:], "seq", SLICES)
    head_sinks = lax.dynamic_slice_in_dim(sinks, part * (sinks.shape[0] // SLICES), sinks.shape[0] // SLICES, 0)
    attended = attend(first[None], head_sinks, q, jnp.concatenate([kv_tail, kv], axis=1))

    core, row = part % 2, part // 2
    order = jnp.stack(
        [
            (row ^ r) * 2 * tp + (core ^ c) * tp + (side ^ t)
            for c in range(2)
            for r in range(2)
            for t in range(tp)
        ]
    ).astype(jnp.int32)
    half = blocks // 2
    result = jnp.zeros((tokens.shape[1], block), jnp.bfloat16)
    for k in range(slabs):
        terms = output_terms(order, weights_out[k], attended)
        from_core = swap(terms[half:], 1, 0)
        sums = terms[:half].astype(jnp.float32) + from_core.astype(jnp.float32)
        sent = sums.astype(jnp.bfloat16)
        total = sums[0]
        total += swap(sent[1], 0, 1).astype(jnp.float32)
        total += swap(sent[2], 2, 0).astype(jnp.float32)
        total += swap(sent[3], 2, 1).astype(jnp.float32)
        depth = total.shape[0]
        result = lax.dynamic_update_slice_in_dim(
            result, total.astype(jnp.bfloat16), slabs_held[k] * depth, 0
        )
    return result.T


def rotary(vectors, places):
    half_dim = vectors.shape[-1] // 2
    angles = angles_of(places).T[:, None, :]
    cosine = jnp.cos(angles)
    sine = jnp.sin(angles)
    lower_half = vectors[..., :half_dim]
    upper_half = vectors[..., half_dim:]
    return jnp.concatenate(
        [lower_half * cosine - upper_half * sine, upper_half * cosine + lower_half * sine], axis=-1
    )


def attend_rows(query_rows, key_value_rows, sink_scores, query_pos, key_pos):
    key_part = key_value_rows[:, :, 0, :]
    value_part = key_value_rows[:, :, 1, :]
    scores = jnp.einsum(
        "qhgd,khd->hgqk", query_rows, key_part, preferred_element_type=jnp.float32
    ) * HEAD_WIDTH ** (-0.5)
    allowed = (
        (key_pos[None, :] <= query_pos[:, None])
        & (key_pos[None, :] > query_pos[:, None] - WINDOW_KEYS)
        & (key_pos[None, :] >= 0)
    )
    scores = jnp.where(allowed[None, None], scores, -jnp.inf)
    row_max = jnp.maximum(jnp.max(scores, axis=-1), sink_scores[:, :, None])
    exponent = jnp.exp(scores - row_max[..., None])
    denominator = jnp.sum(exponent, axis=-1) + jnp.exp(sink_scores[:, :, None] - row_max)
    weights = exponent.astype(jnp.bfloat16)
    mixture = jnp.einsum("hgqk,khd->qhgd", weights, value_part, preferred_element_type=jnp.float32)
    return (mixture / jnp.transpose(denominator, (2, 0, 1))[..., None]).astype(jnp.bfloat16)


def finish(kv_sum, places, kv_heads):
    split_key_value = kv_sum.reshape(kv_sum.shape[0], kv_heads, 2, HEAD_WIDTH)
    key_part = rotary(split_key_value[:, :, 0, :], places)
    return jnp.stack([key_part, split_key_value[:, :, 1, :]], axis=2).astype(jnp.bfloat16)


def row_body(tokens, w_query, w_kv, w_out, sinks):
    token_rows = lax.all_gather(tokens, "tp", axis=0, tiled=True)
    row_count = token_rows.shape[0]
    kv_width = w_kv.shape[1]
    kv_heads = kv_width // (2 * HEAD_WIDTH)
    q_width = w_query.shape[1]
    head_groups = q_width // HEAD_WIDTH // kv_heads
    start_pos = lax.axis_index("seq") * row_count
    query_pos = start_pos + jnp.arange(row_count, dtype=jnp.int32)
    key_pos = start_pos - WINDOW_KEYS + jnp.arange(row_count + WINDOW_KEYS, dtype=jnp.int32)
    query_sum = jnp.dot(
        token_rows,
        lax.all_gather(w_query, "seq", axis=0, tiled=True),
        preferred_element_type=jnp.float32,
    )
    kv_sum = jnp.dot(
        token_rows,
        lax.all_gather(w_kv, "seq", axis=0, tiled=True),
        preferred_element_type=jnp.float32,
    )
    query_rows = rotary(
        query_sum.reshape(row_count, kv_heads * head_groups, HEAD_WIDTH), query_pos
    ).astype(jnp.bfloat16)
    query_rows = query_rows.reshape(row_count, kv_heads, head_groups, HEAD_WIDTH)
    local_kv = finish(kv_sum, query_pos, kv_heads).reshape(row_count, kv_width)
    kv_tail = shift(local_kv[row_count - WINDOW_KEYS :], "seq", 1)
    key_value_rows = jnp.concatenate([kv_tail, local_kv], axis=0).reshape(
        row_count + WINDOW_KEYS, kv_heads, 2, HEAD_WIDTH
    )
    attended = attend_rows(
        query_rows, key_value_rows, sinks.reshape(kv_heads, head_groups), query_pos, key_pos
    ).reshape(row_count, q_width)
    out_terms = lax.dot_general(
        attended,
        lax.all_gather(w_out, "seq", axis=0, tiled=True),
        (((1,), (1,)), ((), ())),
        preferred_element_type=jnp.float32,
    )
    return lax.psum_scatter(out_terms.astype(jnp.bfloat16), "tp", scatter_dimension=0, tiled=True)


def solution(mesh):
    in_specs = (P(("seq", "tp"), None), P("seq", "tp"), P("seq", "tp"), P("seq", "tp"), P("tp"))
    out_specs = P(("seq", "tp"), None)

    def body(tokens, w_query, w_kv, w_out, sinks):
        by_slabs = (
            w_kv.shape[1] == SLICES * 2 * HEAD_WIDTH
            and mesh.shape["tp"] == 2
            and mesh.shape["seq"] == 4 * SLICES
            and tokens.shape[0] % (2 * WINDOW_KEYS) == 0
            and (w_query.shape[0] * SLICES) % 16 == 0
        )
        return (slab_body if by_slabs else row_body)(tokens, w_query, w_kv, w_out, sinks)

    return jax.shard_map(body, mesh=mesh, in_specs=in_specs, out_specs=out_specs, check_vma=False)
```

```python
import functools
import math

import jax
import jax.numpy as jnp
from jax import lax
from jax.experimental import pallas as pl
from jax.experimental.pallas import tpu as pltpu
from jax.sharding import PartitionSpec as P

HEAD_WIDTH = 64
WINDOW_KEYS = 128
SLICES = 4

rope_base = 150000.0
vmem_bytes = 48 * 1024 * 1024
log2e = math.log2(math.e)
score_scale = HEAD_WIDTH**-0.5 * log2e


def shift(value, axis, by):
    devices = lax.axis_size(axis)
    pairs = [(i, i + by) for i in range(devices) if 0 <= i + by < devices]
    return lax.ppermute(value, axis, pairs)


def angles_of(places):
    half_dim = HEAD_WIDTH // 2
    frequency = jnp.exp(
        jnp.arange(half_dim, dtype=jnp.float32) * (-2.0 * math.log(rope_base) / HEAD_WIDTH)
    )
    return places.astype(jnp.float32)[None, :] * frequency[:, None]


def columns_dot(one, other):
    return lax.dot_general(one, other, (((0,), (0,)), ((), ())), preferred_element_type=jnp.float32)


def gather_project_kernel(zs, *refs, depth, cuts):
    pieces, (w0, w1, w2, total, last, held, sems) = refs[: len(cuts)], refs[len(cuts) :]
    copies = []
    for i, (block, start, rows) in enumerate(cuts):
        copy = pltpu.make_async_copy(pieces[i], held.at[block, pl.ds(start, rows)], sems.at[i])
        copy.start()
        copies.append((block, copy))
    for block in range(held.shape[0]):
        for at, copy in copies:
            if at == block:
                copy.wait()
        term = None
        for k, w in enumerate((w0, w1, w2)):
            rows = pl.ds(pl.multiple_of(zs[k] * depth, 16), depth)
            more = columns_dot(w[...], held[block, rows, :])
            term = more if term is None else term + more
        total[block] = term
        last[block] = held[block, pl.ds(pl.multiple_of(zs[3] * depth, 16), depth), :]


def gather_project(zs, pieces, cuts, weights):
    blocks = 1 + max(at for at, _, _ in cuts)
    features = max(start + rows for _, start, rows in cuts)
    block = pieces[0].shape[1]
    depth, width = weights[0].shape
    return pl.pallas_call(
        functools.partial(gather_project_kernel, depth=depth, cuts=cuts),
        in_specs=[pl.BlockSpec(memory_space=pltpu.SMEM)]
        + [pl.BlockSpec(memory_space=pl.ANY)] * len(pieces)
        + [pl.BlockSpec(memory_space=pltpu.VMEM)] * 3,
        out_specs=[pl.BlockSpec(memory_space=pltpu.VMEM)] * 2,
        out_shape=[
            jax.ShapeDtypeStruct((blocks, width, block), jnp.float32),
            jax.ShapeDtypeStruct((blocks, depth, block), jnp.bfloat16),
        ],
        scratch_shapes=[
            pltpu.VMEM((blocks, features, block), jnp.bfloat16),
            pltpu.SemaphoreType.DMA((len(pieces),)),
        ],
        compiler_params=pltpu.CompilerParams(vmem_limit_bytes=vmem_bytes),
        cost_estimate=pl.CostEstimate(
            flops=6 * width * depth * blocks * block,
            bytes_accessed=2 * features * blocks * block,
            transcendentals=0,
        ),
        name="gather_project",
    )(zs, *pieces, *weights)


def project_kernel(order, before_a, before_b, last_a, last_b, w, cosine, sine, kv_out, q_out):
    half = HEAD_WIDTH // 2
    block = before_a.shape[2]
    step = before_a.shape[0] + before_b.shape[0]
    for at in range(step):
        before, last = ((before_a, last_a), (before_b, last_b))[at // before_a.shape[0]]
        i = at % before_a.shape[0]
        total = before[i] + columns_dot(w[...], last[i])
        place = order[pl.program_id(0) * step + at]
        lanes = pl.ds(pl.multiple_of(place * block, block), block)
        cos, sin = cosine[:, lanes], sine[:, lanes]

        def rotated(at_row):
            lower, upper = total[at_row : at_row + half], total[at_row + half : at_row + 2 * half]
            return jnp.concatenate([lower * cos - upper * sin, upper * cos + lower * sin], axis=0)

        kv_out[0:HEAD_WIDTH, lanes] = rotated(0).astype(jnp.bfloat16)
        kv_out[HEAD_WIDTH : 2 * HEAD_WIDTH, lanes] = total[HEAD_WIDTH : 2 * HEAD_WIDTH].astype(jnp.bfloat16)
        for h in range(q_out.shape[1] // HEAD_WIDTH):
            q_out[place, h * HEAD_WIDTH : (h + 1) * HEAD_WIDTH] = (
                rotated((h + 2) * HEAD_WIDTH) * score_scale
            ).astype(jnp.bfloat16)


def project(order, before, last, w, cosine, sine):
    blocks, depth, block = last[0].shape
    blocks *= 2
    width = w.shape[1]
    kv_width = 2 * HEAD_WIDTH
    pair = lambda *shape: pl.BlockSpec((2, *shape), lambda j, order: (j, 0, 0))
    whole = lambda *shape: pl.BlockSpec(shape, lambda j, order: (0,) * len(shape))
    angle = whole(HEAD_WIDTH // 2, blocks * block)
    return pl.pallas_call(
        project_kernel,
        grid_spec=pltpu.PrefetchScalarGridSpec(
            num_scalar_prefetch=1,
            grid=(2,),
            in_specs=[
                pair(width, block),
                pair(width, block),
                pair(depth, block),
                pair(depth, block),
                whole(depth, width),
                angle,
                angle,
            ],
            out_specs=[whole(kv_width, blocks * block), whole(blocks, width - kv_width, block)],
        ),
        out_shape=[
            jax.ShapeDtypeStruct((kv_width, blocks * block), jnp.bfloat16),
            jax.ShapeDtypeStruct((blocks, width - kv_width, block), jnp.bfloat16),
        ],
        compiler_params=pltpu.CompilerParams(vmem_limit_bytes=vmem_bytes),
        cost_estimate=pl.CostEstimate(
            flops=2 * width * depth * blocks * block,
            bytes_accessed=2 * depth * (blocks * block + width),
            transcendentals=0,
        ),
        name="project",
    )(order, *before, *last, w, cosine, sine)


def attend_kernel(first, sinks, q, kv, *refs, low):
    *tail, give, keep, keys, values = refs
    window = WINDOW_KEYS
    width, block = q.shape[1:]
    heads = width // HEAD_WIDTH
    parts = block // window
    span = 4 * block
    if tail:
        keys[:window] = jnp.transpose(tail[0][:HEAD_WIDTH])
        values[:, :window] = tail[0][HEAD_WIDTH:]
        keys[window:] = jnp.transpose(kv[:HEAD_WIDTH, low : low + span])
        values[:, window:] = kv[HEAD_WIDTH:, low : low + span]
    else:
        keys[...] = jnp.transpose(kv[:HEAD_WIDTH, low - window : low + span])
        values[...] = kv[HEAD_WIDTH:, low - window : low + span]

    row = lax.broadcasted_iota(jnp.int32, (2 * window, window), 0)
    lane = lax.broadcasted_iota(jnp.int32, (2 * window, window), 1)
    seen = (row > lane) & (row <= lane + window)
    left = lax.broadcasted_iota(jnp.int32, (1, 2 * window), 1) < window
    core = first[1]
    units = [(mine, side, part) for mine in range(2) for side in range(2) for part in range(parts)]

    def at_block(unit):
        mine, side, _ = unit
        return (core if mine else 1 - core) * 2 + side

    def at_token(unit):
        return pl.multiple_of(at_block(unit) * block + unit[2] * window, window)

    def bias_of(unit):
        allowed = seen
        if tail and unit[1:] == (0, 0):
            allowed = seen & (row >= jnp.where(first[0] + at_block(unit) == 0, window, 0))
        bias = jnp.where(allowed, 0.0, -jnp.inf)
        return jnp.concatenate([bias, bias], axis=1)

    def scores_of(unit):
        lanes = slice(unit[2] * window, (unit[2] + 1) * window)
        key_rows = keys[pl.ds(at_token(unit), 2 * window), :]
        out = []
        for h in range(0, heads, 2):
            rows = slice(h * HEAD_WIDTH, (h + 1) * HEAD_WIDTH), slice((h + 1) * HEAD_WIDTH, (h + 2) * HEAD_WIDTH)
            pair = jnp.concatenate([q[at_block(unit), r, lanes] for r in rows], axis=1)
            out.append(jnp.dot(key_rows, pair, preferred_element_type=jnp.float32))
        return out

    def weights_of(unit, scores):
        bias = bias_of(unit)
        out = []
        for i, score in enumerate(scores):
            score = score + bias
            sink = jnp.where(left, sinks[2 * i], sinks[2 * i + 1]) * log2e
            top = jnp.maximum(jnp.max(score, axis=0, keepdims=True), sink)
            exponent = jnp.exp2(score - top)
            denominator = jnp.sum(exponent, axis=0, keepdims=True) + jnp.exp2(sink - top)
            out.append((exponent.astype(jnp.bfloat16), 1.0 / denominator))
        return out

    def mix(unit, weights):
        mine, side, part = unit
        lanes = slice(part * window, (part + 1) * window)
        value_rows = values[:, pl.ds(at_token(unit), 2 * window)]
        out = keep if mine else give
        for i, (weight, scale) in enumerate(weights):
            mixture = jnp.dot(value_rows, weight, preferred_element_type=jnp.float32)
            result = (mixture * scale).astype(jnp.bfloat16)
            for j in range(2):
                rows = slice((2 * i + j) * HEAD_WIDTH, (2 * i + j + 1) * HEAD_WIDTH)
                out[side, rows, lanes] = result[:, j * window : (j + 1) * window]

    ahead = scores_of(units[0])
    behind = None
    for n, unit in enumerate(units):
        scores = ahead
        if n + 1 < len(units):
            ahead = scores_of(units[n + 1])
        weights = weights_of(unit, scores)
        if behind is not None:
            mix(*behind)
        behind = unit, weights
    mix(*behind)


def attend(first, sinks, q, kv, half, tail=()):
    _, width, block = q.shape
    window = WINDOW_KEYS
    return pl.pallas_call(
        functools.partial(attend_kernel, low=half * 4 * block),
        grid_spec=pltpu.PrefetchScalarGridSpec(
            num_scalar_prefetch=2,
            grid=(1,),
            in_specs=[pl.BlockSpec((4, width, block), lambda i, *_: (half, 0, 0))]
            + [pl.BlockSpec(x.shape, lambda i, *_: (0, 0)) for x in (kv, *tail)],
            out_specs=[pl.BlockSpec((2, width, block), lambda i, *_: (0, 0, 0))] * 2,
            scratch_shapes=[
                pltpu.VMEM((4 * block + window, HEAD_WIDTH), jnp.bfloat16),
                pltpu.VMEM((HEAD_WIDTH, 4 * block + window), jnp.bfloat16),
            ],
        ),
        out_shape=[jax.ShapeDtypeStruct((2, width, block), jnp.bfloat16)] * 2,
        compiler_params=pltpu.CompilerParams(vmem_limit_bytes=vmem_bytes),
        cost_estimate=pl.CostEstimate(
            flops=32 * width * block * window, bytes_accessed=16 * width * block, transcendentals=0
        ),
        name="attend",
    )(first, sinks, q, kv, *tail)


def sums_kernel(sides, w_near, w_far, near0, near1, far0, far1, own, to_x, to_y, cross_a, cross_b):
    row, side = sides[0], sides[1]
    middle = cross_a.shape[0]

    def of(near, far, place):
        total = jnp.dot(w_near[...], near[place], preferred_element_type=jnp.float32)
        return total + jnp.dot(w_far[...], far[place], preferred_element_type=jnp.float32)

    def all_of(mine, other):
        cross = of(*other, 1 - side).astype(jnp.bfloat16)
        cross_a[...] = cross[:middle]
        cross_b[...] = cross[middle:]
        to_x[...] = of(*mine, 1 - side).astype(jnp.bfloat16)
        to_y[...] = of(*other, side).astype(jnp.bfloat16)
        own[...] = of(*mine, side)

    @pl.when(row == 0)
    def _():
        all_of((near0, far0), (near1, far1))

    @pl.when(row == 1)
    def _():
        all_of((near1, far1), (near0, far0))


def output_sums(sides, w_near, w_far, near, far):
    depth = w_near.shape[0]
    block = near[0].shape[2]
    vmem = pl.BlockSpec(memory_space=pltpu.VMEM)
    bf16 = lambda rows: jax.ShapeDtypeStruct((rows, block), jnp.bfloat16)
    return pl.pallas_call(
        sums_kernel,
        in_specs=[pl.BlockSpec(memory_space=pltpu.SMEM)] + [vmem] * 6,
        out_specs=[vmem] * 5,
        out_shape=[
            jax.ShapeDtypeStruct((depth, block), jnp.float32),
            bf16(depth),
            bf16(depth),
            bf16(depth // 2),
            bf16(depth - depth // 2),
        ],
        compiler_params=pltpu.CompilerParams(vmem_limit_bytes=vmem_bytes),
        cost_estimate=pl.CostEstimate(
            flops=16 * w_near.shape[1] * depth * block,
            bytes_accessed=16 * depth * block,
            transcendentals=0,
        ),
        name="output_sums",
    )(sides, w_near, w_far, *near, *far)


def slab_body(tokens, w_query, w_kv, w_out, sinks):
    devices = lax.axis_size("seq")
    slabs = devices // SLICES
    tp = lax.axis_size("tp")
    place = lax.axis_index("seq")
    slab, part = place // SLICES, place % SLICES
    side = lax.axis_index("tp")
    block = tokens.shape[0]
    blocks = SLICES * tp
    both = ("seq", "tp")

    def swap(value, flip_seq, flip_tp):
        pairs = [
            (s * tp + t, (s ^ flip_seq) * tp + (t ^ flip_tp)) for s in range(devices) for t in range(tp)
        ]
        return lax.ppermute(value, both, pairs)

    def turn(value):
        pairs = [(s, (s + SLICES) % devices) for s in range(devices)]
        return lax.ppermute(value, "seq", pairs)

    tie = lambda *values: lax.optimization_barrier(values)

    core, row = part % 2, part // 2
    order = jnp.stack(
        [
            (row ^ r) * 2 * tp + (core ^ c) * tp + (side ^ t)
            for c in range(2)
            for r in range(2)
            for t in range(tp)
        ]
    ).astype(jnp.int32)

    def of_head(weight, head):
        width = weight.shape[1] // SLICES
        return lax.dynamic_slice_in_dim(weight, head * width, width, 1)

    def by(flag, one, other):
        joined = jnp.concatenate([one, other], axis=0)
        return jnp.where(flag == 1, jnp.concatenate([other, one], axis=0), joined)

    def of_chip(make):
        return by(core, make(part), swap(make(part ^ 1), 1, 0))

    def of_next_chip(make):
        return by(core, swap(make(part ^ 2), 2, 0), swap(make(part ^ 3), 3, 0))

    def in_head(head):
        return jnp.concatenate([of_head(w_kv, head), of_head(w_query, head)], axis=1)

    def out_head(head):
        return of_head(w_out, head)

    own = tokens.T
    features = own.shape[0]
    upper = features // 2
    near, far = [of_chip(in_head)], [of_next_chip(in_head)]
    near.append(turn(near[0]))
    from_x = swap(own[:upper], 0, 1), swap(own[upper:], 0, 1)
    near[1], far[0], own_late = tie(near[1], far[0], own)
    far.append(turn(far[0]))
    near.append(turn(near[1]))
    from_y = swap(own_late[:upper], 2, 0), swap(own_late[upper:], 2, 0)
    far.append(turn(far[1]))
    near.append(turn(near[2]))
    far.append(turn(far[2]))
    diagonal = swap(from_x[0], 2, 0), swap(from_y[1], 0, 1)
    weights_in = [by(row, n, f) for n, f in zip(near[:-1], far[:-1])]

    first = slab * (blocks * block)
    places = first + jnp.arange(blocks * block, dtype=jnp.int32)
    angles = angles_of(places)
    slabs_held = (slab - jnp.arange(slabs, dtype=jnp.int32)) % slabs
    whole = (0, 0, features)
    parts = [(0, upper), (upper, features - upper)]
    before_a, last_a = gather_project(
        slabs_held,
        [own, *from_x, swap(own, 1, 0), *(swap(x, 1, 0) for x in from_x)],
        [whole, *((1, *p) for p in parts), (2, *whole[1:]), *((3, *p) for p in parts)],
        weights_in,
    )
    before_b, last_b = gather_project(
        slabs_held,
        [*from_y, *diagonal, *(swap(x, 1, 0) for x in (*from_y, *diagonal))],
        [(at, *p) for at in range(4) for p in parts],
        weights_in,
    )

    near_out, far_out = [of_chip(out_head)], [of_next_chip(out_head)]
    near_out[0], far[-1] = tie(near_out[0], far[-1])
    near_out.append(turn(near_out[0]))
    kv, q = project(order, (before_a, before_b), (last_a, last_b), by(row, near[-1], far[-1]), jnp.cos(angles), jnp.sin(angles))
    kv_tail = shift(kv[:, -WINDOW_KEYS:], "seq", SLICES)
    heads = sinks.shape[0] // SLICES
    head_sinks = lax.dynamic_slice_in_dim(sinks, part * heads, heads, 0)
    first_row = jnp.stack([first, core])
    mixed = [None, attend(first_row, head_sinks, q, kv, 1)]
    q, near_out[1], far_out[0] = tie(q, near_out[1], far_out[0])
    far_out.append(turn(far_out[0]))
    near_out.append(turn(near_out[1]))
    mixed[0] = attend(first_row, head_sinks, q, kv, 0, (kv_tail,))
    came = [swap(give, 1, 0) for give, _ in mixed]
    kept = [keep for _, keep in mixed]

    sides = jnp.stack([row, side])
    depth = 2 * near_out[0].shape[0]
    middle = depth // 2
    result = jnp.zeros((features, block), jnp.bfloat16)
    for k in range(slabs):
        weight = by(row, near_out[k], far_out[k])
        total, to_x, to_y, cross_a, cross_b = output_sums(sides, weight, swap(weight, 1, 0), kept, came)
        if k == 0:
            total, near_out[2], far_out[1] = tie(total, near_out[2], far_out[1])
            far_out.append(turn(far_out[1]))
            near_out.append(turn(near_out[2]))
            far_out.append(turn(far_out[2]))
        by_x = swap(cross_a, 0, 1).astype(jnp.float32)
        by_y = swap(cross_b, 2, 0).astype(jnp.float32)
        to_x = jnp.concatenate([to_x[:middle], (to_x[middle:].astype(jnp.float32) + by_y).astype(jnp.bfloat16)], axis=0)
        to_y = jnp.concatenate([(to_y[:middle].astype(jnp.float32) + by_x).astype(jnp.bfloat16), to_y[middle:]], axis=0)
        total += swap(to_x, 0, 1).astype(jnp.float32)
        total += swap(to_y, 2, 0).astype(jnp.float32)
        result = lax.dynamic_update_slice_in_dim(result, total.astype(jnp.bfloat16), slabs_held[k] * depth, 0)
    return result.T


def rotary(vectors, places):
    half_dim = vectors.shape[-1] // 2
    angles = angles_of(places).T[:, None, :]
    cosine = jnp.cos(angles)
    sine = jnp.sin(angles)
    lower_half = vectors[..., :half_dim]
    upper_half = vectors[..., half_dim:]
    return jnp.concatenate(
        [lower_half * cosine - upper_half * sine, upper_half * cosine + lower_half * sine], axis=-1
    )


def attend_rows(query_rows, key_value_rows, sink_scores, query_pos, key_pos):
    key_part = key_value_rows[:, :, 0, :]
    value_part = key_value_rows[:, :, 1, :]
    scores = jnp.einsum(
        "qhgd,khd->hgqk", query_rows, key_part, preferred_element_type=jnp.float32
    ) * HEAD_WIDTH ** (-0.5)
    allowed = (
        (key_pos[None, :] <= query_pos[:, None])
        & (key_pos[None, :] > query_pos[:, None] - WINDOW_KEYS)
        & (key_pos[None, :] >= 0)
    )
    scores = jnp.where(allowed[None, None], scores, -jnp.inf)
    row_max = jnp.maximum(jnp.max(scores, axis=-1), sink_scores[:, :, None])
    exponent = jnp.exp(scores - row_max[..., None])
    denominator = jnp.sum(exponent, axis=-1) + jnp.exp(sink_scores[:, :, None] - row_max)
    weights = exponent.astype(jnp.bfloat16)
    mixture = jnp.einsum("hgqk,khd->qhgd", weights, value_part, preferred_element_type=jnp.float32)
    return (mixture / jnp.transpose(denominator, (2, 0, 1))[..., None]).astype(jnp.bfloat16)


def finish(kv_sum, places, kv_heads):
    split_key_value = kv_sum.reshape(kv_sum.shape[0], kv_heads, 2, HEAD_WIDTH)
    key_part = rotary(split_key_value[:, :, 0, :], places)
    return jnp.stack([key_part, split_key_value[:, :, 1, :]], axis=2).astype(jnp.bfloat16)


def row_body(tokens, w_query, w_kv, w_out, sinks):
    token_rows = lax.all_gather(tokens, "tp", axis=0, tiled=True)
    row_count = token_rows.shape[0]
    kv_width = w_kv.shape[1]
    kv_heads = kv_width // (2 * HEAD_WIDTH)
    q_width = w_query.shape[1]
    head_groups = q_width // HEAD_WIDTH // kv_heads
    start_pos = lax.axis_index("seq") * row_count
    query_pos = start_pos + jnp.arange(row_count, dtype=jnp.int32)
    key_pos = start_pos - WINDOW_KEYS + jnp.arange(row_count + WINDOW_KEYS, dtype=jnp.int32)
    query_sum = jnp.dot(
        token_rows,
        lax.all_gather(w_query, "seq", axis=0, tiled=True),
        preferred_element_type=jnp.float32,
    )
    kv_sum = jnp.dot(
        token_rows,
        lax.all_gather(w_kv, "seq", axis=0, tiled=True),
        preferred_element_type=jnp.float32,
    )
    query_rows = rotary(
        query_sum.reshape(row_count, kv_heads * head_groups, HEAD_WIDTH), query_pos
    ).astype(jnp.bfloat16)
    query_rows = query_rows.reshape(row_count, kv_heads, head_groups, HEAD_WIDTH)
    local_kv = finish(kv_sum, query_pos, kv_heads).reshape(row_count, kv_width)
    kv_tail = shift(local_kv[row_count - WINDOW_KEYS :], "seq", 1)
    key_value_rows = jnp.concatenate([kv_tail, local_kv], axis=0).reshape(
        row_count + WINDOW_KEYS, kv_heads, 2, HEAD_WIDTH
    )
    attended = attend_rows(
        query_rows, key_value_rows, sinks.reshape(kv_heads, head_groups), query_pos, key_pos
    ).reshape(row_count, q_width)
    out_terms = lax.dot_general(
        attended,
        lax.all_gather(w_out, "seq", axis=0, tiled=True),
        (((1,), (1,)), ((), ())),
        preferred_element_type=jnp.float32,
    )
    return lax.psum_scatter(out_terms.astype(jnp.bfloat16), "tp", scatter_dimension=0, tiled=True)


def solution(mesh):
    in_specs = (P(("seq", "tp"), None), P("seq", "tp"), P("seq", "tp"), P("seq", "tp"), P("tp"))
    out_specs = P(("seq", "tp"), None)

    def body(tokens, w_query, w_kv, w_out, sinks):
        by_slabs = (
            w_kv.shape[1] == SLICES * 2 * HEAD_WIDTH
            and mesh.shape["tp"] == 2
            and mesh.shape["seq"] == 4 * SLICES
            and tokens.shape[0] % (2 * WINDOW_KEYS) == 0
            and (w_query.shape[0] * SLICES) % 16 == 0
        )
        return (slab_body if by_slabs else row_body)(tokens, w_query, w_kv, w_out, sinks)

    return jax.shard_map(body, mesh=mesh, in_specs=in_specs, out_specs=out_specs, check_vma=False)
```

```python
import functools
import math

import jax
import jax.numpy as jnp
from jax import lax
from jax.experimental import pallas as pl
from jax.experimental.pallas import tpu as pltpu
from jax.sharding import PartitionSpec as P

HEAD_WIDTH = 64
WINDOW_KEYS = 128
SLICES = 4

rope_base = 150000.0
vmem_bytes = 48 * 1024 * 1024
wide_vmem_bytes = 62 * 1024 * 1024
log2e = math.log2(math.e)
small_cost = pl.CostEstimate(flops=1000, bytes_accessed=1000, transcendentals=0)
score_scale = HEAD_WIDTH**-0.5 * log2e


def shift(value, axis, by):
    devices = lax.axis_size(axis)
    pairs = [(i, i + by) for i in range(devices) if 0 <= i + by < devices]
    return lax.ppermute(value, axis, pairs)


def angles_of(places):
    half_dim = HEAD_WIDTH // 2
    frequency = jnp.exp(
        jnp.arange(half_dim, dtype=jnp.float32) * (-2.0 * math.log(rope_base) / HEAD_WIDTH)
    )
    return places.astype(jnp.float32)[None, :] * frequency[:, None]


def columns_dot(one, other):
    return lax.dot_general(one, other, (((0,), (0,)), ((), ())), preferred_element_type=jnp.float32)


def project_kernel(zs, order, *refs, cuts):
    slabs = zs.shape[0]
    pieces, weights = refs[: len(cuts)], refs[len(cuts) : -8]
    cosine, sine, kv_out, q_out, tail_out, held, w_held, sems = refs[-8:]
    pairs, features, lanes = held.shape
    depth, block, half = features // slabs, lanes // 2, HEAD_WIDTH // 2
    loads = []
    row = 0
    for i, w in enumerate(weights):
        rows = pl.ds(pl.multiple_of(zs[row // depth] * depth + row % depth, 16), w.shape[0])
        loads.append((0, pltpu.make_async_copy(w, w_held.at[rows], sems.at[len(cuts) + i])))
        row += w.shape[0]
    for i, (at, start, rows) in enumerate(cuts):
        target = held.at[at // 2, pl.ds(start, rows), pl.ds(at % 2 * block, block)]
        loads.append((at // 2, pltpu.make_async_copy(pieces[i], target, sems.at[i])))
    for _, load in loads:
        load.start()

    def product_of(pair):
        for at, load in loads:
            if at == pair:
                load.wait()
        return columns_dot(w_held[...], held[pair])

    def finish_of(pair, product):
        for side in range(2):
            place = order[2 * pair + side]
            total = product[:, side * block : (side + 1) * block]
            lanes = pl.ds(pl.multiple_of(place * block, block), block)
            cos, sin = cosine[:, lanes], sine[:, lanes]

            def rotated(at):
                lower, upper = total[at : at + half], total[at + half : at + 2 * half]
                return jnp.concatenate([lower * cos - upper * sin, upper * cos + lower * sin], axis=0)

            kv_out[0:HEAD_WIDTH, lanes] = rotated(0).astype(jnp.bfloat16)
            kv_out[HEAD_WIDTH : 2 * HEAD_WIDTH, lanes] = total[HEAD_WIDTH : 2 * HEAD_WIDTH].astype(jnp.bfloat16)
            for h in range(q_out.shape[1] // HEAD_WIDTH):
                q_out[place, h * HEAD_WIDTH : (h + 1) * HEAD_WIDTH] = (
                    rotated((h + 2) * HEAD_WIDTH) * score_scale
                ).astype(jnp.bfloat16)

    ahead = product_of(0)
    for pair in range(pairs):
        product = ahead
        if pair + 1 < pairs:
            ahead = product_of(pair + 1)
        finish_of(pair, product)
    tail_out[...] = kv_out[:, kv_out.shape[1] - WINDOW_KEYS :]


def project(zs, order, pieces, weights, cosine, sine):
    (features, width), block = (sum(w.shape[0] for w in weights), weights[0].shape[1]), pieces[0].shape[1]
    blocks = order.shape[0]
    kv_width = 2 * HEAD_WIDTH
    cuts, at, start = [], 0, 0
    for piece in pieces:
        cuts.append((at, start, piece.shape[0]))
        at, start = (at, start + piece.shape[0]) if start + piece.shape[0] < features else (at + 1, 0)
    vmem = pl.BlockSpec(memory_space=pltpu.VMEM)
    return pl.pallas_call(
        functools.partial(project_kernel, cuts=cuts),
        in_specs=[pl.BlockSpec(memory_space=pltpu.SMEM)] * 2
        + [pl.BlockSpec(memory_space=pl.ANY)] * (len(pieces) + len(weights))
        + [vmem] * 2,
        out_specs=[vmem] * 3,
        out_shape=[
            jax.ShapeDtypeStruct((kv_width, blocks * block), jnp.bfloat16),
            jax.ShapeDtypeStruct((blocks, width - kv_width, block), jnp.bfloat16),
            jax.ShapeDtypeStruct((kv_width, WINDOW_KEYS), jnp.bfloat16),
        ],
        scratch_shapes=[
            pltpu.VMEM((blocks // 2, features, 2 * block), jnp.bfloat16),
            pltpu.VMEM((features, width), jnp.bfloat16),
            pltpu.SemaphoreType.DMA((len(pieces) + len(weights),)),
        ],
        compiler_params=pltpu.CompilerParams(vmem_limit_bytes=wide_vmem_bytes),
        cost_estimate=small_cost,
        name="project",
    )(zs, order, *pieces, *weights, cosine, sine)


def attend_kernel(first, sinks, q, kv, *refs, low):
    *tail, give, keep, keys, values = refs
    window = WINDOW_KEYS
    width, block = q.shape[1:]
    heads = width // HEAD_WIDTH
    parts = block // window
    span = 4 * block
    if tail:
        keys[:window] = jnp.transpose(tail[0][:HEAD_WIDTH])
        values[:, :window] = tail[0][HEAD_WIDTH:]
        keys[window:] = jnp.transpose(kv[:HEAD_WIDTH, low : low + span])
        values[:, window:] = kv[HEAD_WIDTH:, low : low + span]
    else:
        keys[...] = jnp.transpose(kv[:HEAD_WIDTH, low - window : low + span])
        values[...] = kv[HEAD_WIDTH:, low - window : low + span]

    row = lax.broadcasted_iota(jnp.int32, (2 * window, window), 0)
    lane = lax.broadcasted_iota(jnp.int32, (2 * window, window), 1)
    seen = (row > lane) & (row <= lane + window)
    left = lax.broadcasted_iota(jnp.int32, (1, 2 * window), 1) < window
    core = first[1]
    units = [(mine, side, part) for mine in range(2) for side in range(2) for part in range(parts)]

    def at_block(unit):
        mine, side, _ = unit
        return (core if mine else 1 - core) * 2 + side

    def at_token(unit):
        return pl.multiple_of(at_block(unit) * block + unit[2] * window, window)

    def bias_of(unit):
        allowed = seen
        if tail and unit[1:] == (0, 0):
            allowed = seen & (row >= jnp.where(first[0] + at_block(unit) == 0, window, 0))
        bias = jnp.where(allowed, 0.0, -jnp.inf)
        return jnp.concatenate([bias, bias], axis=1)

    def scores_of(unit):
        lanes = slice(unit[2] * window, (unit[2] + 1) * window)
        key_rows = keys[pl.ds(at_token(unit), 2 * window), :]
        out = []
        for h in range(0, heads, 2):
            rows = slice(h * HEAD_WIDTH, (h + 1) * HEAD_WIDTH), slice((h + 1) * HEAD_WIDTH, (h + 2) * HEAD_WIDTH)
            pair = jnp.concatenate([q[at_block(unit), r, lanes] for r in rows], axis=1)
            out.append(jnp.dot(key_rows, pair, preferred_element_type=jnp.float32))
        return out

    def weights_of(unit, scores):
        bias = bias_of(unit)
        out = []
        for i, score in enumerate(scores):
            score = score + bias
            sink = jnp.where(left, sinks[2 * i], sinks[2 * i + 1]) * log2e
            top = jnp.maximum(jnp.max(score, axis=0, keepdims=True), sink)
            exponent = jnp.exp2(score - top)
            denominator = jnp.sum(exponent, axis=0, keepdims=True) + jnp.exp2(sink - top)
            out.append((exponent.astype(jnp.bfloat16), 1.0 / denominator))
        return out

    def mix(unit, weights):
        mine, side, part = unit
        lanes = slice(part * window, (part + 1) * window)
        value_rows = values[:, pl.ds(at_token(unit), 2 * window)]
        out = keep if mine else give
        for i, (weight, scale) in enumerate(weights):
            mixture = jnp.dot(value_rows, weight, preferred_element_type=jnp.float32)
            result = (mixture * scale).astype(jnp.bfloat16)
            for j in range(2):
                rows = slice((2 * i + j) * HEAD_WIDTH, (2 * i + j + 1) * HEAD_WIDTH)
                out[side, rows, lanes] = result[:, j * window : (j + 1) * window]

    ahead = scores_of(units[0])
    behind = None
    for n, unit in enumerate(units):
        scores = ahead
        if n + 1 < len(units):
            ahead = scores_of(units[n + 1])
        weights = weights_of(unit, scores)
        if behind is not None:
            mix(*behind)
        behind = unit, weights
    mix(*behind)


def attend(first, sinks, q, kv, half, tail=()):
    _, width, block = q.shape
    window = WINDOW_KEYS
    return pl.pallas_call(
        functools.partial(attend_kernel, low=half * 4 * block),
        grid_spec=pltpu.PrefetchScalarGridSpec(
            num_scalar_prefetch=2,
            grid=(1,),
            in_specs=[pl.BlockSpec((4, width, block), lambda i, *_: (half, 0, 0))]
            + [pl.BlockSpec(x.shape, lambda i, *_: (0, 0)) for x in (kv, *tail)],
            out_specs=[pl.BlockSpec((2, width, block), lambda i, *_: (0, 0, 0))] * 2,
            scratch_shapes=[
                pltpu.VMEM((4 * block + window, HEAD_WIDTH), jnp.bfloat16),
                pltpu.VMEM((HEAD_WIDTH, 4 * block + window), jnp.bfloat16),
            ],
        ),
        out_shape=[jax.ShapeDtypeStruct((2, width, block), jnp.bfloat16)] * 2,
        compiler_params=pltpu.CompilerParams(vmem_limit_bytes=vmem_bytes),
        cost_estimate=small_cost,
        name="attend",
    )(first, sinks, q, kv, *tail)


def first_part(weights):
    rows = weights[0].shape[0]
    return rows if len(weights) > 1 else rows // 32 * 16 + 16


def sums_kernel(sides, *refs, count, crossing):
    weights, (near0, near1, far0, far1), outs = refs[: 2 * count], refs[2 * count : 2 * count + 4], refs[2 * count + 4 :]
    row, side = sides[0], sides[1]
    middle = outs[0].shape[0]

    def all_of(mine, other):
        start = 0
        for w_near, w_far in zip(weights[:count], weights[count:]):

            def write(halves, place, top, bottom, w_near=w_near, w_far=w_far, start=start):
                near, far = halves
                total = jnp.dot(w_near[...], near[place], preferred_element_type=jnp.float32)
                total += jnp.dot(w_far[...], far[place], preferred_element_type=jnp.float32)
                if count > 1:
                    out = bottom if start else top
                    out[...] = total.astype(out.dtype)
                else:
                    top[...] = total[:middle].astype(top.dtype)
                    bottom[...] = total[middle:].astype(bottom.dtype)

            if crossing:
                write(other, 1 - side, *outs)
            else:
                write(mine, 1 - side, *outs[2:4])
                write(other, side, *outs[4:6])
                write(mine, side, *outs[:2])
            start += w_near.shape[0]

    @pl.when(row == 0)
    def _():
        all_of((near0, far0), (near1, far1))

    @pl.when(row == 1)
    def _():
        all_of((near1, far1), (near0, far0))


def output_sums(sides, w_near, w_far, near, far, crossing):
    depth = sum(w.shape[0] for w in w_near)
    middle = first_part(w_near)
    block = near[0].shape[2]
    vmem = pl.BlockSpec(memory_space=pltpu.VMEM)
    types = [jnp.bfloat16] * 2
    if not crossing:
        types = [jnp.float32, jnp.float32, jnp.bfloat16, jnp.float32, jnp.float32, jnp.bfloat16]
    return pl.pallas_call(
        functools.partial(sums_kernel, count=len(w_near), crossing=crossing),
        in_specs=[pl.BlockSpec(memory_space=pltpu.SMEM)] + [vmem] * (2 * len(w_near) + 4),
        out_specs=[vmem] * len(types),
        out_shape=[
            jax.ShapeDtypeStruct((depth - middle if i % 2 else middle, block), kind) for i, kind in enumerate(types)
        ],
        compiler_params=pltpu.CompilerParams(vmem_limit_bytes=vmem_bytes),
        cost_estimate=small_cost,
        name="crossing_sums" if crossing else "output_sums",
    )(sides, *w_near, *w_far, *near, *far)


def slab_body(tokens, w_query, w_kv, w_out, sinks):
    devices = lax.axis_size("seq")
    slabs = devices // SLICES
    tp = lax.axis_size("tp")
    place = lax.axis_index("seq")
    slab, part = place // SLICES, place % SLICES
    side = lax.axis_index("tp")
    block = tokens.shape[0]
    blocks = SLICES * tp
    both = ("seq", "tp")

    def swap(value, flip_seq, flip_tp):
        pairs = [
            (s * tp + t, (s ^ flip_seq) * tp + (t ^ flip_tp)) for s in range(devices) for t in range(tp)
        ]
        return lax.ppermute(value, both, pairs)

    def turn(value):
        pairs = [(s, (s + SLICES) % devices) for s in range(devices)]
        return lax.ppermute(value, "seq", pairs)

    tie = lambda *values: lax.optimization_barrier(values)

    core, row = part % 2, part // 2
    def of_head(weight, head):
        width = weight.shape[1] // SLICES
        return lax.dynamic_slice_in_dim(weight, head * width, width, 1)

    def by(flag, one, other):
        joined = jnp.concatenate([one, other], axis=0)
        return jnp.where(flag == 1, jnp.concatenate([other, one], axis=0), joined)

    def of_chip(make):
        return by(core, make(part), swap(make(part ^ 1), 1, 0))

    def of_next_chip(make):
        return [swap(make(part ^ 2), 2, 0), swap(make(part ^ 3), 3, 0)]

    def in_head(head):
        return jnp.concatenate([of_head(w_kv, head), of_head(w_query, head)], axis=1)

    def out_head(head):
        return of_head(w_out, head)

    order = jnp.stack(
        [
            (row ^ r) * 2 * tp + (core ^ c) * tp + (side ^ t)
            for r in range(2)
            for c in range(2)
            for t in range(tp)
        ]
    ).astype(jnp.int32)

    own = tokens.T
    features = own.shape[0]
    third = features // 3
    near, far = of_chip(in_head), of_next_chip(in_head)
    near, own_late = tie(near, own)
    a, b, c = (own_late[i * third : (i + 1) * third] for i in range(3))
    next_near = turn(near)
    *far, x_a = tie(*far, swap(a, 0, 1))
    far = by(core, *far)
    weights_in = [by(row, near, far)]
    near, far, x_a, a, b, c = tie(next_near, far, x_a, a, b, c)
    far, x_b, y_b, near, x_a, a, c = tie(turn(far), swap(b, 0, 1), swap(b, 2, 0), near, x_a, a, c)
    weights_in.append(by(row, near, far))
    weight = turn(weights_in[1])
    first = slab * (blocks * block)
    places = first + jnp.arange(blocks * block, dtype=jnp.int32)
    angles = angles_of(places)
    cosine, sine = jnp.cos(angles), jnp.sin(angles)
    slabs_held = jnp.stack([(slab - k) % slabs for k in range(slabs)]).astype(jnp.int32)
    sides = jnp.stack([row, side])
    first_row = jnp.stack([first, core])
    heads = sinks.shape[0] // SLICES
    head_sinks = lax.dynamic_slice_in_dim(sinks, part * heads, heads, 0)
    small = [cosine, sine, slabs_held, order, sides, first_row, head_sinks]
    x_c, y_c, x_a, y_b, a, weights_in[0], *small = tie(
        swap(c, 0, 1), swap(c, 2, 0), x_a, y_b, a, weights_in[0], *small
    )
    cosine, sine, slabs_held, order, sides, first_row, head_sinks = small
    weight, y_a, d_b, x_a, y_c = tie(weight, swap(a, 2, 0), swap(y_b, 0, 1), x_a, y_c)
    cut = weight.shape[0] // 32 * 16 + 16
    weights_in += [weight, turn(weight[:cut]), weight[cut:]]
    d_a, d_c, w_out, *weights_in[-2:] = tie(swap(x_a, 2, 0), swap(y_c, 0, 1), w_out, *weights_in[-2:])
    weights_in[-1] = turn(weights_in[-1])

    def of_cores(*pieces):
        return [*pieces, *(swap(piece, 1, 0) for piece in pieces)]

    pieces = of_cores(own, x_a, x_b, x_c) + of_cores(y_a, y_b, y_c, d_a, d_b, d_c)
    near_out = of_chip(out_head)
    far_out = of_next_chip(out_head)
    *pieces, far_out[0], far_out[1] = tie(*pieces, *far_out)
    own_out = by(row, near_out, by(core, *far_out))
    own_out_late, weights_in[-1] = tie(own_out, weights_in[-1])
    weights_out = [own_out, turn(own_out_late)]
    kv, q, kv_tail = project(slabs_held, order, pieces, weights_in, cosine, sine)
    kv_tail = shift(kv_tail, "seq", SLICES)
    mixed = [None, list(attend(first_row, head_sinks, q, kv, 1))]
    mixed[1][1], kv_tail, weights_out[1] = tie(mixed[1][1], kv_tail, weights_out[1])
    mixed[0] = attend(first_row, head_sinks, q, kv, 0, (kv_tail,))
    came = [swap(give, 1, 0) for give, _ in mixed]
    kept = [keep for _, keep in mixed]

    depth = weights_out[0].shape[0]
    result = jnp.zeros((features, block), jnp.bfloat16)
    weights_out.append(turn(weights_out[1]))
    chunks = ((0, 1), (2,), (3,))
    sums, plain, merged = [], [], []
    for n, chunk in enumerate(chunks):
        w_near = [weights_out[k] for k in chunk]
        w_far = [swap(w, 1, 0) for w in w_near]
        crosses = output_sums(sides, w_near, w_far, kept, came, True)
        by_x, by_y = swap(crosses[0], 0, 1), swap(crosses[1], 2, 0)
        *own_sums, x_top, x_bottom, y_top, y_bottom = output_sums(sides, w_near, w_far, kept, came, False)
        if n == 0:
            own_sums[0], weights_out[2] = tie(own_sums[0], weights_out[2])
            weights_out.append(turn(weights_out[2]))
        plain.append([swap(x_top, 0, 1), swap(y_bottom, 2, 0)])
        if n:
            by_x, by_y, *merged[n - 1] = tie(by_x, by_y, *merged[n - 1])
        else:
            by_x, by_y = tie(by_x, by_y)
        y_top = (y_top + by_x.astype(jnp.float32)).astype(jnp.bfloat16)
        x_bottom = (x_bottom + by_y.astype(jnp.float32)).astype(jnp.bfloat16)
        if n + 1 < len(chunks):
            kept[0], *plain[n] = tie(kept[0], *plain[n])
        merged.append([swap(x_bottom, 0, 1), swap(y_top, 2, 0)])
        sums.append(own_sums)
    for n, chunk in enumerate(chunks):
        top = sums[n][0] + plain[n][0].astype(jnp.float32) + merged[n][1].astype(jnp.float32)
        bottom = sums[n][1] + merged[n][0].astype(jnp.float32) + plain[n][1].astype(jnp.float32)
        place = (slab - chunk[0]) % slabs * depth
        result = lax.dynamic_update_slice_in_dim(result, top.astype(jnp.bfloat16), place, 0)
        place = (slab - chunk[1]) % slabs * depth if len(chunk) > 1 else place + top.shape[0]
        result = lax.dynamic_update_slice_in_dim(result, bottom.astype(jnp.bfloat16), place, 0)
    return result.T


def rotary(vectors, places):
    half_dim = vectors.shape[-1] // 2
    angles = angles_of(places).T[:, None, :]
    cosine = jnp.cos(angles)
    sine = jnp.sin(angles)
    lower_half = vectors[..., :half_dim]
    upper_half = vectors[..., half_dim:]
    return jnp.concatenate(
        [lower_half * cosine - upper_half * sine, upper_half * cosine + lower_half * sine], axis=-1
    )


def attend_rows(query_rows, key_value_rows, sink_scores, query_pos, key_pos):
    key_part = key_value_rows[:, :, 0, :]
    value_part = key_value_rows[:, :, 1, :]
    scores = jnp.einsum(
        "qhgd,khd->hgqk", query_rows, key_part, preferred_element_type=jnp.float32
    ) * HEAD_WIDTH ** (-0.5)
    allowed = (
        (key_pos[None, :] <= query_pos[:, None])
        & (key_pos[None, :] > query_pos[:, None] - WINDOW_KEYS)
        & (key_pos[None, :] >= 0)
    )
    scores = jnp.where(allowed[None, None], scores, -jnp.inf)
    row_max = jnp.maximum(jnp.max(scores, axis=-1), sink_scores[:, :, None])
    exponent = jnp.exp(scores - row_max[..., None])
    denominator = jnp.sum(exponent, axis=-1) + jnp.exp(sink_scores[:, :, None] - row_max)
    weights = exponent.astype(jnp.bfloat16)
    mixture = jnp.einsum("hgqk,khd->qhgd", weights, value_part, preferred_element_type=jnp.float32)
    return (mixture / jnp.transpose(denominator, (2, 0, 1))[..., None]).astype(jnp.bfloat16)


def finish(kv_sum, places, kv_heads):
    split_key_value = kv_sum.reshape(kv_sum.shape[0], kv_heads, 2, HEAD_WIDTH)
    key_part = rotary(split_key_value[:, :, 0, :], places)
    return jnp.stack([key_part, split_key_value[:, :, 1, :]], axis=2).astype(jnp.bfloat16)


def row_body(tokens, w_query, w_kv, w_out, sinks):
    token_rows = lax.all_gather(tokens, "tp", axis=0, tiled=True)
    row_count = token_rows.shape[0]
    kv_width = w_kv.shape[1]
    kv_heads = kv_width // (2 * HEAD_WIDTH)
    q_width = w_query.shape[1]
    head_groups = q_width // HEAD_WIDTH // kv_heads
    start_pos = lax.axis_index("seq") * row_count
    query_pos = start_pos + jnp.arange(row_count, dtype=jnp.int32)
    key_pos = start_pos - WINDOW_KEYS + jnp.arange(row_count + WINDOW_KEYS, dtype=jnp.int32)
    query_sum = jnp.dot(
        token_rows,
        lax.all_gather(w_query, "seq", axis=0, tiled=True),
        preferred_element_type=jnp.float32,
    )
    kv_sum = jnp.dot(
        token_rows,
        lax.all_gather(w_kv, "seq", axis=0, tiled=True),
        preferred_element_type=jnp.float32,
    )
    query_rows = rotary(
        query_sum.reshape(row_count, kv_heads * head_groups, HEAD_WIDTH), query_pos
    ).astype(jnp.bfloat16)
    query_rows = query_rows.reshape(row_count, kv_heads, head_groups, HEAD_WIDTH)
    local_kv = finish(kv_sum, query_pos, kv_heads).reshape(row_count, kv_width)
    kv_tail = shift(local_kv[row_count - WINDOW_KEYS :], "seq", 1)
    key_value_rows = jnp.concatenate([kv_tail, local_kv], axis=0).reshape(
        row_count + WINDOW_KEYS, kv_heads, 2, HEAD_WIDTH
    )
    attended = attend_rows(
        query_rows, key_value_rows, sinks.reshape(kv_heads, head_groups), query_pos, key_pos
    ).reshape(row_count, q_width)
    out_terms = lax.dot_general(
        attended,
        lax.all_gather(w_out, "seq", axis=0, tiled=True),
        (((1,), (1,)), ((), ())),
        preferred_element_type=jnp.float32,
    )
    return lax.psum_scatter(out_terms.astype(jnp.bfloat16), "tp", scatter_dimension=0, tiled=True)


def solution(mesh):
    in_specs = (P(("seq", "tp"), None), P("seq", "tp"), P("seq", "tp"), P("seq", "tp"), P("tp"))
    out_specs = P(("seq", "tp"), None)

    def body(tokens, w_query, w_kv, w_out, sinks):
        by_slabs = (
            w_kv.shape[1] == SLICES * 2 * HEAD_WIDTH
            and mesh.shape["tp"] == 2
            and mesh.shape["seq"] == 4 * SLICES
            and tokens.shape[0] % (2 * WINDOW_KEYS) == 0
            and (w_query.shape[0] * SLICES) % 16 == 0
        )
        return (slab_body if by_slabs else row_body)(tokens, w_query, w_kv, w_out, sinks)

    return jax.shard_map(body, mesh=mesh, in_specs=in_specs, out_specs=out_specs, check_vma=False)
```

```python
import functools
import math

import jax
import jax.numpy as jnp
from jax import lax
from jax.experimental import pallas as pl
from jax.experimental.pallas import tpu as pltpu
from jax.sharding import PartitionSpec as P

HEAD_WIDTH = 64
WINDOW_KEYS = 128
SLICES = 4

rope_base = 150000.0
vmem_bytes = 48 * 1024 * 1024
wide_vmem_bytes = 62 * 1024 * 1024
log2e = math.log2(math.e)
small_cost = pl.CostEstimate(flops=1000, bytes_accessed=1000, transcendentals=0)
score_scale = HEAD_WIDTH**-0.5 * log2e


def shift(value, axis, by):
    devices = lax.axis_size(axis)
    pairs = [(i, i + by) for i in range(devices) if 0 <= i + by < devices]
    return lax.ppermute(value, axis, pairs)


def angles_of(places):
    half_dim = HEAD_WIDTH // 2
    frequency = jnp.exp(
        jnp.arange(half_dim, dtype=jnp.float32) * (-2.0 * math.log(rope_base) / HEAD_WIDTH)
    )
    return places.astype(jnp.float32)[None, :] * frequency[:, None]


def columns_dot(one, other):
    return lax.dot_general(one, other, (((0,), (0,)), ((), ())), preferred_element_type=jnp.float32)


def attend_kernel(first, sinks, q, kv, *refs, low):
    *tail, give, keep, keys, values = refs
    attend_blocks(first, sinks, q, kv, tail, give, keep, keys, values, low, 0)


def attend_blocks(first, sinks, q, kv, tail, give, keep, keys, values, low, base):
    window = WINDOW_KEYS
    width, block = q.shape[1:]
    heads = width // HEAD_WIDTH
    parts = block // window
    span = 4 * block
    if tail:
        keys[:window] = jnp.transpose(tail[0][:HEAD_WIDTH])
        values[:, :window] = tail[0][HEAD_WIDTH:]
        keys[window:] = jnp.transpose(kv[:HEAD_WIDTH, low : low + span])
        values[:, window:] = kv[HEAD_WIDTH:, low : low + span]
    else:
        keys[...] = jnp.transpose(kv[:HEAD_WIDTH, low - window : low + span])
        values[...] = kv[HEAD_WIDTH:, low - window : low + span]

    row = lax.broadcasted_iota(jnp.int32, (2 * window, window), 0)
    lane = lax.broadcasted_iota(jnp.int32, (2 * window, window), 1)
    seen = (row > lane) & (row <= lane + window)
    left = lax.broadcasted_iota(jnp.int32, (1, 2 * window), 1) < window
    core = first[1]
    units = [(mine, side, part) for mine in range(2) for side in range(2) for part in range(parts)]

    def at_block(unit):
        mine, side, _ = unit
        return (core if mine else 1 - core) * 2 + side

    def at_token(unit):
        return pl.multiple_of(at_block(unit) * block + unit[2] * window, window)

    def bias_of(unit):
        allowed = seen
        if tail and unit[1:] == (0, 0):
            allowed = seen & (row >= jnp.where(first[0] + at_block(unit) == 0, window, 0))
        bias = jnp.where(allowed, 0.0, -jnp.inf)
        return jnp.concatenate([bias, bias], axis=1)

    def scores_of(unit):
        lanes = slice(unit[2] * window, (unit[2] + 1) * window)
        key_rows = keys[pl.ds(at_token(unit), 2 * window), :]
        out = []
        for h in range(0, heads, 2):
            rows = slice(h * HEAD_WIDTH, (h + 1) * HEAD_WIDTH), slice((h + 1) * HEAD_WIDTH, (h + 2) * HEAD_WIDTH)
            pair = jnp.concatenate([q[base + at_block(unit), r, lanes] for r in rows], axis=1)
            out.append(jnp.dot(key_rows, pair, preferred_element_type=jnp.float32))
        return out

    def weights_of(unit, scores):
        bias = bias_of(unit)
        out = []
        for i, score in enumerate(scores):
            score = score + bias
            sink = jnp.where(left, sinks[2 * i], sinks[2 * i + 1]) * log2e
            top = jnp.maximum(jnp.max(score, axis=0, keepdims=True), sink)
            exponent = jnp.exp2(score - top)
            denominator = jnp.sum(exponent, axis=0, keepdims=True) + jnp.exp2(sink - top)
            out.append((exponent.astype(jnp.bfloat16), 1.0 / denominator))
        return out

    def mix(unit, weights):
        mine, side, part = unit
        lanes = slice(part * window, (part + 1) * window)
        value_rows = values[:, pl.ds(at_token(unit), 2 * window)]
        out = keep if mine else give
        for i, (weight, scale) in enumerate(weights):
            mixture = jnp.dot(value_rows, weight, preferred_element_type=jnp.float32)
            result = (mixture * scale).astype(jnp.bfloat16)
            for j in range(2):
                rows = slice((2 * i + j) * HEAD_WIDTH, (2 * i + j + 1) * HEAD_WIDTH)
                out[side, rows, lanes] = result[:, j * window : (j + 1) * window]

    ahead = scores_of(units[0])
    behind = None
    for n, unit in enumerate(units):
        scores = ahead
        if n + 1 < len(units):
            ahead = scores_of(units[n + 1])
        weights = weights_of(unit, scores)
        if behind is not None:
            mix(*behind)
        behind = unit, weights
    mix(*behind)


def attend(first, sinks, q, kv, half, tail=()):
    _, width, block = q.shape
    window = WINDOW_KEYS
    return pl.pallas_call(
        functools.partial(attend_kernel, low=half * 4 * block),
        grid_spec=pltpu.PrefetchScalarGridSpec(
            num_scalar_prefetch=2,
            grid=(1,),
            in_specs=[pl.BlockSpec((4, width, block), lambda i, *_: (half, 0, 0))]
            + [pl.BlockSpec(x.shape, lambda i, *_: (0, 0)) for x in (kv, *tail)],
            out_specs=[pl.BlockSpec((2, width, block), lambda i, *_: (0, 0, 0))] * 2,
            scratch_shapes=[
                pltpu.VMEM((4 * block + window, HEAD_WIDTH), jnp.bfloat16),
                pltpu.VMEM((HEAD_WIDTH, 4 * block + window), jnp.bfloat16),
            ],
        ),
        out_shape=[jax.ShapeDtypeStruct((2, width, block), jnp.bfloat16)] * 2,
        compiler_params=pltpu.CompilerParams(vmem_limit_bytes=vmem_bytes),
        cost_estimate=small_cost,
        name="attend",
    )(first, sinks, q, kv, *tail)


def project_kernel(zs, order, first, sinks, *refs, cuts):
    slabs = zs.shape[0]
    pieces, weights = refs[: len(cuts)], refs[len(cuts) : -14]
    cosine, sine, kv_low, q_low, tail_out, give, keep, held, w_held, kv_out, q_out, keys, values, sems = refs[-14:]
    pairs, features, lanes = held.shape
    depth, block, half = features // slabs, lanes // 2, HEAD_WIDTH // 2
    loads = []
    row = 0
    for i, w in enumerate(weights):
        rows = pl.ds(pl.multiple_of(zs[row // depth] * depth + row % depth, 16), w.shape[0])
        loads.append((0, pltpu.make_async_copy(w, w_held.at[rows], sems.at[len(cuts) + i])))
        row += w.shape[0]
    for i, (at, start, rows) in enumerate(cuts):
        target = held.at[at // 2, pl.ds(start, rows), pl.ds(at % 2 * block, block)]
        loads.append((at // 2, pltpu.make_async_copy(pieces[i], target, sems.at[i])))
    for _, load in loads:
        load.start()

    def product_of(pair):
        for at, load in loads:
            if at == pair:
                load.wait()
        return columns_dot(w_held[...], held[pair])

    def finish_of(pair, product):
        for side in range(2):
            place = order[2 * pair + side]
            total = product[:, side * block : (side + 1) * block]
            lanes = pl.ds(pl.multiple_of(place * block, block), block)
            cos, sin = cosine[:, lanes], sine[:, lanes]

            def rotated(at):
                lower, upper = total[at : at + half], total[at + half : at + 2 * half]
                return jnp.concatenate([lower * cos - upper * sin, upper * cos + lower * sin], axis=0)

            kv_out[0:HEAD_WIDTH, lanes] = rotated(0).astype(jnp.bfloat16)
            kv_out[HEAD_WIDTH : 2 * HEAD_WIDTH, lanes] = total[HEAD_WIDTH : 2 * HEAD_WIDTH].astype(jnp.bfloat16)
            for h in range(q_out.shape[1] // HEAD_WIDTH):
                q_out[place, h * HEAD_WIDTH : (h + 1) * HEAD_WIDTH] = (
                    rotated((h + 2) * HEAD_WIDTH) * score_scale
                ).astype(jnp.bfloat16)

    ahead = product_of(0)
    for pair in range(pairs):
        product = ahead
        if pair + 1 < pairs:
            ahead = product_of(pair + 1)
        finish_of(pair, product)
    tail_out[...] = kv_out[:, kv_out.shape[1] - WINDOW_KEYS :]
    kv_low[...] = kv_out[:, : kv_low.shape[1]]
    q_low[...] = q_out[: q_low.shape[0]]
    attend_blocks(first, sinks, q_out, kv_out, (), give, keep, keys, values, pairs * block, pairs)


def project(zs, order, first, sinks, pieces, weights, cosine, sine):
    (features, width), block = (sum(w.shape[0] for w in weights), weights[0].shape[1]), pieces[0].shape[1]
    blocks = order.shape[0]
    kv_width = 2 * HEAD_WIDTH
    cuts, at, start = [], 0, 0
    for piece in pieces:
        cuts.append((at, start, piece.shape[0]))
        at, start = (at, start + piece.shape[0]) if start + piece.shape[0] < features else (at + 1, 0)
    vmem = pl.BlockSpec(memory_space=pltpu.VMEM)
    return pl.pallas_call(
        functools.partial(project_kernel, cuts=cuts),
        in_specs=[pl.BlockSpec(memory_space=pltpu.SMEM)] * 4
        + [pl.BlockSpec(memory_space=pl.ANY)] * (len(pieces) + len(weights))
        + [vmem] * 2,
        out_specs=[vmem] * 5,
        out_shape=[
            jax.ShapeDtypeStruct((kv_width, blocks // 2 * block), jnp.bfloat16),
            jax.ShapeDtypeStruct((blocks // 2, width - kv_width, block), jnp.bfloat16),
            jax.ShapeDtypeStruct((kv_width, WINDOW_KEYS), jnp.bfloat16),
            *[jax.ShapeDtypeStruct((blocks // 4, width - kv_width, block), jnp.bfloat16)] * 2,
        ],
        scratch_shapes=[
            pltpu.VMEM((blocks // 2, features, 2 * block), jnp.bfloat16),
            pltpu.VMEM((features, width), jnp.bfloat16),
            pltpu.VMEM((kv_width, blocks * block), jnp.bfloat16),
            pltpu.VMEM((blocks, width - kv_width, block), jnp.bfloat16),
            pltpu.VMEM((blocks // 2 * block + WINDOW_KEYS, HEAD_WIDTH), jnp.bfloat16),
            pltpu.VMEM((HEAD_WIDTH, blocks // 2 * block + WINDOW_KEYS), jnp.bfloat16),
            pltpu.SemaphoreType.DMA((len(pieces) + len(weights),)),
        ],
        compiler_params=pltpu.CompilerParams(vmem_limit_bytes=wide_vmem_bytes),
        cost_estimate=small_cost,
        name="project",
    )(zs, order, first, sinks, *pieces, *weights, cosine, sine)


def first_part(weights):
    rows = weights[0].shape[0]
    return rows if len(weights) > 1 else rows // 32 * 16 + 16


def sums_kernel(sides, *refs, count, crossing):
    weights, (near0, near1, far0, far1), outs = refs[: 2 * count], refs[2 * count : 2 * count + 4], refs[2 * count + 4 :]
    row, side = sides[0], sides[1]
    middle = outs[0].shape[0]

    def all_of(mine, other):
        start = 0
        for w_near, w_far in zip(weights[:count], weights[count:]):

            def write(halves, place, top, bottom, w_near=w_near, w_far=w_far, start=start):
                near, far = halves
                total = jnp.dot(w_near[...], near[place], preferred_element_type=jnp.float32)
                total += jnp.dot(w_far[...], far[place], preferred_element_type=jnp.float32)
                if count > 1:
                    out = bottom if start else top
                    out[...] = total.astype(out.dtype)
                else:
                    top[...] = total[:middle].astype(top.dtype)
                    bottom[...] = total[middle:].astype(bottom.dtype)

            if crossing:
                write(other, 1 - side, *outs)
            else:
                write(mine, 1 - side, *outs[2:4])
                write(other, side, *outs[4:6])
                write(mine, side, *outs[:2])
            start += w_near.shape[0]

    @pl.when(row == 0)
    def _():
        all_of((near0, far0), (near1, far1))

    @pl.when(row == 1)
    def _():
        all_of((near1, far1), (near0, far0))


def output_sums(sides, w_near, w_far, near, far, crossing):
    depth = sum(w.shape[0] for w in w_near)
    middle = first_part(w_near)
    block = near[0].shape[2]
    vmem = pl.BlockSpec(memory_space=pltpu.VMEM)
    types = [jnp.bfloat16] * 2
    if not crossing:
        types = [jnp.float32, jnp.float32, jnp.bfloat16, jnp.float32, jnp.float32, jnp.bfloat16]
    return pl.pallas_call(
        functools.partial(sums_kernel, count=len(w_near), crossing=crossing),
        in_specs=[pl.BlockSpec(memory_space=pltpu.SMEM)] + [vmem] * (2 * len(w_near) + 4),
        out_specs=[vmem] * len(types),
        out_shape=[
            jax.ShapeDtypeStruct((depth - middle if i % 2 else middle, block), kind) for i, kind in enumerate(types)
        ],
        compiler_params=pltpu.CompilerParams(vmem_limit_bytes=vmem_bytes),
        cost_estimate=small_cost,
        name="crossing_sums" if crossing else "output_sums",
    )(sides, *w_near, *w_far, *near, *far)


def slab_body(tokens, w_query, w_kv, w_out, sinks):
    devices = lax.axis_size("seq")
    slabs = devices // SLICES
    tp = lax.axis_size("tp")
    place = lax.axis_index("seq")
    slab, part = place // SLICES, place % SLICES
    side = lax.axis_index("tp")
    block = tokens.shape[0]
    blocks = SLICES * tp
    both = ("seq", "tp")

    def swap(value, flip_seq, flip_tp):
        pairs = [
            (s * tp + t, (s ^ flip_seq) * tp + (t ^ flip_tp)) for s in range(devices) for t in range(tp)
        ]
        return lax.ppermute(value, both, pairs)

    def turn(value):
        pairs = [(s, (s + SLICES) % devices) for s in range(devices)]
        return lax.ppermute(value, "seq", pairs)

    tie = lambda *values: lax.optimization_barrier(values)

    core, row = part % 2, part // 2
    def of_head(weight, head):
        width = weight.shape[1] // SLICES
        return lax.dynamic_slice_in_dim(weight, head * width, width, 1)

    def by(flag, one, other):
        joined = jnp.concatenate([one, other], axis=0)
        return jnp.where(flag == 1, jnp.concatenate([other, one], axis=0), joined)

    def of_chip(make):
        return by(core, make(part), swap(make(part ^ 1), 1, 0))

    def of_next_chip(make):
        return [swap(make(part ^ 2), 2, 0), swap(make(part ^ 3), 3, 0)]

    def in_head(head):
        return jnp.concatenate([of_head(w_kv, head), of_head(w_query, head)], axis=1)

    def out_head(head):
        return of_head(w_out, head)

    order = jnp.stack(
        [
            (row ^ r) * 2 * tp + (core ^ c) * tp + (side ^ t)
            for r in range(2)
            for c in range(2)
            for t in range(tp)
        ]
    ).astype(jnp.int32)

    own = tokens.T
    features = own.shape[0]
    third = features // 3
    near, far = of_chip(in_head), of_next_chip(in_head)
    near, own_late = tie(near, own)
    a, b, c = (own_late[i * third : (i + 1) * third] for i in range(3))
    next_near = turn(near)
    *far, x_a = tie(*far, swap(a, 0, 1))
    far = by(core, *far)
    weights_in = [by(row, near, far)]
    near, far, x_a, a, b, c = tie(next_near, far, x_a, a, b, c)
    far, x_b, y_b, near, x_a, a, c = tie(turn(far), swap(b, 0, 1), swap(b, 2, 0), near, x_a, a, c)
    weights_in.append(by(row, near, far))
    weight = turn(weights_in[1])
    first = slab * (blocks * block)
    places = first + jnp.arange(blocks * block, dtype=jnp.int32)
    angles = angles_of(places)
    cosine, sine = jnp.cos(angles), jnp.sin(angles)
    slabs_held = jnp.stack([(slab - k) % slabs for k in range(slabs)]).astype(jnp.int32)
    sides = jnp.stack([row, side])
    first_row = jnp.stack([first, core])
    heads = sinks.shape[0] // SLICES
    head_sinks = lax.dynamic_slice_in_dim(sinks, part * heads, heads, 0)
    small = [cosine, sine, slabs_held, order, sides, first_row, head_sinks]
    x_c, y_c, x_a, y_b, a, weights_in[0], *small = tie(
        swap(c, 0, 1), swap(c, 2, 0), x_a, y_b, a, weights_in[0], *small
    )
    cosine, sine, slabs_held, order, sides, first_row, head_sinks = small
    weight, y_a, d_b, x_a, y_c = tie(weight, swap(a, 2, 0), swap(y_b, 0, 1), x_a, y_c)
    cut = weight.shape[0] // 32 * 16 + 16
    weights_in += [weight, turn(weight[:cut]), weight[cut:]]
    d_a, d_c, w_out, *weights_in[-2:] = tie(swap(x_a, 2, 0), swap(y_c, 0, 1), w_out, *weights_in[-2:])
    weights_in[-1] = turn(weights_in[-1])

    def of_cores(*pieces):
        return [*pieces, *(swap(piece, 1, 0) for piece in pieces)]

    pieces = of_cores(own, x_a, x_b, x_c) + of_cores(y_a, y_b, y_c, d_a, d_b, d_c)
    near_out = of_chip(out_head)
    far_out = of_next_chip(out_head)
    *pieces, far_out[0], far_out[1] = tie(*pieces, *far_out)
    own_out = by(row, near_out, by(core, *far_out))
    own_out_late, weights_in[-1] = tie(own_out, weights_in[-1])
    weights_out = [own_out, turn(own_out_late)]
    kv, q, kv_tail, *later = project(slabs_held, order, first_row, head_sinks, pieces, weights_in, cosine, sine)
    kv_tail = shift(kv_tail, "seq", SLICES)
    kv_tail, weights_out[1] = tie(kv_tail, weights_out[1])
    mixed = [None, later]
    mixed[0] = attend(first_row, head_sinks, q, kv, 0, (kv_tail,))
    came = [swap(give, 1, 0) for give, _ in mixed]
    kept = [keep for _, keep in mixed]

    depth = weights_out[0].shape[0]
    result = jnp.zeros((features, block), jnp.bfloat16)
    weights_out.append(turn(weights_out[1]))
    chunks = ((0, 1), (2,), (3,))
    sums, plain, merged = [], [], []
    for n, chunk in enumerate(chunks):
        w_near = [weights_out[k] for k in chunk]
        w_far = [swap(w, 1, 0) for w in w_near]
        crosses = output_sums(sides, w_near, w_far, kept, came, True)
        by_x, by_y = swap(crosses[0], 0, 1), swap(crosses[1], 2, 0)
        *own_sums, x_top, x_bottom, y_top, y_bottom = output_sums(sides, w_near, w_far, kept, came, False)
        if n == 0:
            own_sums[0], weights_out[2] = tie(own_sums[0], weights_out[2])
            weights_out.append(turn(weights_out[2]))
        plain.append([swap(x_top, 0, 1), swap(y_bottom, 2, 0)])
        if n:
            by_x, by_y, *merged[n - 1] = tie(by_x, by_y, *merged[n - 1])
        else:
            by_x, by_y = tie(by_x, by_y)
        y_top = (y_top + by_x.astype(jnp.float32)).astype(jnp.bfloat16)
        x_bottom = (x_bottom + by_y.astype(jnp.float32)).astype(jnp.bfloat16)
        if n + 1 < len(chunks):
            kept[0], *plain[n] = tie(kept[0], *plain[n])
        merged.append([swap(x_bottom, 0, 1), swap(y_top, 2, 0)])
        sums.append(own_sums)
    for n, chunk in enumerate(chunks):
        top = sums[n][0] + plain[n][0].astype(jnp.float32) + merged[n][1].astype(jnp.float32)
        bottom = sums[n][1] + merged[n][0].astype(jnp.float32) + plain[n][1].astype(jnp.float32)
        place = (slab - chunk[0]) % slabs * depth
        result = lax.dynamic_update_slice_in_dim(result, top.astype(jnp.bfloat16), place, 0)
        place = (slab - chunk[1]) % slabs * depth if len(chunk) > 1 else place + top.shape[0]
        result = lax.dynamic_update_slice_in_dim(result, bottom.astype(jnp.bfloat16), place, 0)
    return result.T


def rotary(vectors, places):
    half_dim = vectors.shape[-1] // 2
    angles = angles_of(places).T[:, None, :]
    cosine = jnp.cos(angles)
    sine = jnp.sin(angles)
    lower_half = vectors[..., :half_dim]
    upper_half = vectors[..., half_dim:]
    return jnp.concatenate(
        [lower_half * cosine - upper_half * sine, upper_half * cosine + lower_half * sine], axis=-1
    )


def attend_rows(query_rows, key_value_rows, sink_scores, query_pos, key_pos):
    key_part = key_value_rows[:, :, 0, :]
    value_part = key_value_rows[:, :, 1, :]
    scores = jnp.einsum(
        "qhgd,khd->hgqk", query_rows, key_part, preferred_element_type=jnp.float32
    ) * HEAD_WIDTH ** (-0.5)
    allowed = (
        (key_pos[None, :] <= query_pos[:, None])
        & (key_pos[None, :] > query_pos[:, None] - WINDOW_KEYS)
        & (key_pos[None, :] >= 0)
    )
    scores = jnp.where(allowed[None, None], scores, -jnp.inf)
    row_max = jnp.maximum(jnp.max(scores, axis=-1), sink_scores[:, :, None])
    exponent = jnp.exp(scores - row_max[..., None])
    denominator = jnp.sum(exponent, axis=-1) + jnp.exp(sink_scores[:, :, None] - row_max)
    weights = exponent.astype(jnp.bfloat16)
    mixture = jnp.einsum("hgqk,khd->qhgd", weights, value_part, preferred_element_type=jnp.float32)
    return (mixture / jnp.transpose(denominator, (2, 0, 1))[..., None]).astype(jnp.bfloat16)


def finish(kv_sum, places, kv_heads):
    split_key_value = kv_sum.reshape(kv_sum.shape[0], kv_heads, 2, HEAD_WIDTH)
    key_part = rotary(split_key_value[:, :, 0, :], places)
    return jnp.stack([key_part, split_key_value[:, :, 1, :]], axis=2).astype(jnp.bfloat16)


def row_body(tokens, w_query, w_kv, w_out, sinks):
    token_rows = lax.all_gather(tokens, "tp", axis=0, tiled=True)
    row_count = token_rows.shape[0]
    kv_width = w_kv.shape[1]
    kv_heads = kv_width // (2 * HEAD_WIDTH)
    q_width = w_query.shape[1]
    head_groups = q_width // HEAD_WIDTH // kv_heads
    start_pos = lax.axis_index("seq") * row_count
    query_pos = start_pos + jnp.arange(row_count, dtype=jnp.int32)
    key_pos = start_pos - WINDOW_KEYS + jnp.arange(row_count + WINDOW_KEYS, dtype=jnp.int32)
    query_sum = jnp.dot(
        token_rows,
        lax.all_gather(w_query, "seq", axis=0, tiled=True),
        preferred_element_type=jnp.float32,
    )
    kv_sum = jnp.dot(
        token_rows,
        lax.all_gather(w_kv, "seq", axis=0, tiled=True),
        preferred_element_type=jnp.float32,
    )
    query_rows = rotary(
        query_sum.reshape(row_count, kv_heads * head_groups, HEAD_WIDTH), query_pos
    ).astype(jnp.bfloat16)
    query_rows = query_rows.reshape(row_count, kv_heads, head_groups, HEAD_WIDTH)
    local_kv = finish(kv_sum, query_pos, kv_heads).reshape(row_count, kv_width)
    kv_tail = shift(local_kv[row_count - WINDOW_KEYS :], "seq", 1)
    key_value_rows = jnp.concatenate([kv_tail, local_kv], axis=0).reshape(
        row_count + WINDOW_KEYS, kv_heads, 2, HEAD_WIDTH
    )
    attended = attend_rows(
        query_rows, key_value_rows, sinks.reshape(kv_heads, head_groups), query_pos, key_pos
    ).reshape(row_count, q_width)
    out_terms = lax.dot_general(
        attended,
        lax.all_gather(w_out, "seq", axis=0, tiled=True),
        (((1,), (1,)), ((), ())),
        preferred_element_type=jnp.float32,
    )
    return lax.psum_scatter(out_terms.astype(jnp.bfloat16), "tp", scatter_dimension=0, tiled=True)


def solution(mesh):
    in_specs = (P(("seq", "tp"), None), P("seq", "tp"), P("seq", "tp"), P("seq", "tp"), P("tp"))
    out_specs = P(("seq", "tp"), None)

    def body(tokens, w_query, w_kv, w_out, sinks):
        by_slabs = (
            w_kv.shape[1] == SLICES * 2 * HEAD_WIDTH
            and mesh.shape["tp"] == 2
            and mesh.shape["seq"] == 4 * SLICES
            and tokens.shape[0] % (2 * WINDOW_KEYS) == 0
            and (w_query.shape[0] * SLICES) % 16 == 0
        )
        return (slab_body if by_slabs else row_body)(tokens, w_query, w_kv, w_out, sinks)

    return jax.shard_map(body, mesh=mesh, in_specs=in_specs, out_specs=out_specs, check_vma=False)
```

```python
import functools
import math

import jax
import jax.numpy as jnp
from jax import lax
from jax.experimental import pallas as pl
from jax.experimental.pallas import tpu as pltpu
from jax.sharding import PartitionSpec as P

HEAD_WIDTH = 64
WINDOW_KEYS = 128
SLICES = 4

rope_base = 150000.0
vmem_bytes = 48 * 1024 * 1024
wide_vmem_bytes = 60 * 1024 * 1024
log2e = math.log2(math.e)
small_cost = pl.CostEstimate(flops=1000, bytes_accessed=1000, transcendentals=0)
score_scale = HEAD_WIDTH**-0.5 * log2e


def shift(value, axis, by):
    devices = lax.axis_size(axis)
    pairs = [(i, i + by) for i in range(devices) if 0 <= i + by < devices]
    return lax.ppermute(value, axis, pairs)


def angles_of(places):
    half_dim = HEAD_WIDTH // 2
    frequency = jnp.exp(
        jnp.arange(half_dim, dtype=jnp.float32) * (-2.0 * math.log(rope_base) / HEAD_WIDTH)
    )
    return places.astype(jnp.float32)[None, :] * frequency[:, None]


def columns_dot(one, other):
    return lax.dot_general(one, other, (((0,), (0,)), ((), ())), preferred_element_type=jnp.float32)


def attend_kernel(first, sinks, q, kv, *refs, low):
    *tail, give, keep, keys, values = refs
    attend_blocks(first, sinks, q, kv, tail, give, keep, keys, values, low, 0)


def attend_blocks(first, sinks, q, kv, tail, give, keep, keys, values, low, base):
    window = WINDOW_KEYS
    width, block = q.shape[1:]
    heads = width // HEAD_WIDTH
    parts = block // window
    span = 4 * block
    if tail:
        keys[:window] = jnp.transpose(tail[0][:HEAD_WIDTH])
        values[:, :window] = tail[0][HEAD_WIDTH:]
        keys[window:] = jnp.transpose(kv[:HEAD_WIDTH, low : low + span])
        values[:, window:] = kv[HEAD_WIDTH:, low : low + span]
    else:
        keys[...] = jnp.transpose(kv[:HEAD_WIDTH, low - window : low + span])
        values[...] = kv[HEAD_WIDTH:, low - window : low + span]

    row = lax.broadcasted_iota(jnp.int32, (2 * window, window), 0)
    lane = lax.broadcasted_iota(jnp.int32, (2 * window, window), 1)
    seen = (row > lane) & (row <= lane + window)
    left = lax.broadcasted_iota(jnp.int32, (1, 2 * window), 1) < window
    core = first[1]
    units = [(mine, side, part) for mine in range(2) for side in range(2) for part in range(parts)]

    def at_block(unit):
        mine, side, _ = unit
        return (core if mine else 1 - core) * 2 + side

    def at_token(unit):
        return pl.multiple_of(at_block(unit) * block + unit[2] * window, window)

    def bias_of(unit):
        allowed = seen
        if tail and unit[1:] == (0, 0):
            allowed = seen & (row >= jnp.where(first[0] + at_block(unit) == 0, window, 0))
        bias = jnp.where(allowed, 0.0, -jnp.inf)
        return jnp.concatenate([bias, bias], axis=1)

    def scores_of(unit):
        lanes = slice(unit[2] * window, (unit[2] + 1) * window)
        key_rows = keys[pl.ds(at_token(unit), 2 * window), :]
        out = []
        for h in range(0, heads, 2):
            rows = slice(h * HEAD_WIDTH, (h + 1) * HEAD_WIDTH), slice((h + 1) * HEAD_WIDTH, (h + 2) * HEAD_WIDTH)
            pair = jnp.concatenate([q[base + at_block(unit), r, lanes] for r in rows], axis=1)
            out.append(jnp.dot(key_rows, pair, preferred_element_type=jnp.float32))
        return out

    def weights_of(unit, scores):
        bias = bias_of(unit)
        out = []
        for i, score in enumerate(scores):
            score = score + bias
            sink = jnp.where(left, sinks[2 * i], sinks[2 * i + 1]) * log2e
            top = jnp.maximum(jnp.max(score, axis=0, keepdims=True), sink)
            exponent = jnp.exp2(score - top)
            denominator = jnp.sum(exponent, axis=0, keepdims=True) + jnp.exp2(sink - top)
            out.append((exponent.astype(jnp.bfloat16), 1.0 / denominator))
        return out

    def mix(unit, weights):
        mine, side, part = unit
        lanes = slice(part * window, (part + 1) * window)
        value_rows = values[:, pl.ds(at_token(unit), 2 * window)]
        out = keep if mine else give
        for i, (weight, scale) in enumerate(weights):
            mixture = jnp.dot(value_rows, weight, preferred_element_type=jnp.float32)
            result = (mixture * scale).astype(jnp.bfloat16)
            for j in range(2):
                rows = slice((2 * i + j) * HEAD_WIDTH, (2 * i + j + 1) * HEAD_WIDTH)
                out[side, rows, lanes] = result[:, j * window : (j + 1) * window]

    ahead = scores_of(units[0])
    behind = None
    for n, unit in enumerate(units):
        scores = ahead
        if n + 1 < len(units):
            ahead = scores_of(units[n + 1])
        weights = weights_of(unit, scores)
        if behind is not None:
            mix(*behind)
        behind = unit, weights
    mix(*behind)


def attend(first, sinks, q, kv, half, tail=()):
    _, width, block = q.shape
    window = WINDOW_KEYS
    return pl.pallas_call(
        functools.partial(attend_kernel, low=half * 4 * block),
        grid_spec=pltpu.PrefetchScalarGridSpec(
            num_scalar_prefetch=2,
            grid=(1,),
            in_specs=[pl.BlockSpec((4, width, block), lambda i, *_: (half, 0, 0))]
            + [pl.BlockSpec(x.shape, lambda i, *_: (0, 0)) for x in (kv, *tail)],
            out_specs=[pl.BlockSpec((2, width, block), lambda i, *_: (0, 0, 0))] * 2,
            scratch_shapes=[
                pltpu.VMEM((4 * block + window, HEAD_WIDTH), jnp.bfloat16),
                pltpu.VMEM((HEAD_WIDTH, 4 * block + window), jnp.bfloat16),
            ],
        ),
        out_shape=[jax.ShapeDtypeStruct((2, width, block), jnp.bfloat16)] * 2,
        compiler_params=pltpu.CompilerParams(vmem_limit_bytes=vmem_bytes),
        cost_estimate=small_cost,
        name="attend",
    )(first, sinks, q, kv, *tail)


def project_kernel(zs, order, first, sinks, *refs, cuts):
    slabs = zs.shape[0]
    pieces, weights = refs[: len(cuts)], refs[len(cuts) : -14]
    cosine, sine, kv_low, q_low, tail_out, give, keep, held, w_held, kv_out, q_out, keys, values, sems = refs[-14:]
    pairs, features, lanes = held.shape
    depth, block, half = features // slabs, lanes // 2, HEAD_WIDTH // 2
    loads = []
    row = 0
    for i, w in enumerate(weights):
        rows = pl.ds(pl.multiple_of(zs[row // depth] * depth + row % depth, 16), w.shape[0])
        loads.append((0, pltpu.make_async_copy(w, w_held.at[rows], sems.at[len(cuts) + i])))
        row += w.shape[0]
    for i, (at, start, rows) in enumerate(cuts):
        target = held.at[at // 2, pl.ds(start, rows), pl.ds(at % 2 * block, block)]
        loads.append((at // 2, pltpu.make_async_copy(pieces[i], target, sems.at[i])))
    for _, load in loads:
        load.start()

    def product_of(pair):
        for at, load in loads:
            if at == pair:
                load.wait()
        return columns_dot(w_held[...], held[pair])

    def finish_of(pair, product):
        for side in range(2):
            place = order[2 * pair + side]
            total = product[:, side * block : (side + 1) * block]
            lanes = pl.ds(pl.multiple_of(place * block, block), block)
            cos, sin = cosine[:, lanes], sine[:, lanes]

            def rotated(at):
                lower, upper = total[at : at + half], total[at + half : at + 2 * half]
                return jnp.concatenate([lower * cos - upper * sin, upper * cos + lower * sin], axis=0)

            kv_out[0:HEAD_WIDTH, lanes] = rotated(0).astype(jnp.bfloat16)
            kv_out[HEAD_WIDTH : 2 * HEAD_WIDTH, lanes] = total[HEAD_WIDTH : 2 * HEAD_WIDTH].astype(jnp.bfloat16)
            for h in range(q_out.shape[1] // HEAD_WIDTH):
                q_out[place, h * HEAD_WIDTH : (h + 1) * HEAD_WIDTH] = (
                    rotated((h + 2) * HEAD_WIDTH) * score_scale
                ).astype(jnp.bfloat16)

    ahead = product_of(0)
    for pair in range(pairs):
        product = ahead
        if pair + 1 < pairs:
            ahead = product_of(pair + 1)
        finish_of(pair, product)
    tail_out[...] = kv_out[:, kv_out.shape[1] - WINDOW_KEYS :]
    kv_low[...] = kv_out[:, : kv_low.shape[1]]
    q_low[...] = q_out[: q_low.shape[0]]
    attend_blocks(first, sinks, q_out, kv_out, (), give, keep, keys, values, pairs * block, pairs)


def project(zs, order, first, sinks, pieces, weights, cosine, sine):
    (features, width), block = (sum(w.shape[0] for w in weights), weights[0].shape[1]), pieces[0].shape[1]
    blocks = order.shape[0]
    kv_width = 2 * HEAD_WIDTH
    cuts, at, start = [], 0, 0
    for piece in pieces:
        cuts.append((at, start, piece.shape[0]))
        at, start = (at, start + piece.shape[0]) if start + piece.shape[0] < features else (at + 1, 0)
    vmem = pl.BlockSpec(memory_space=pltpu.VMEM)
    return pl.pallas_call(
        functools.partial(project_kernel, cuts=cuts),
        in_specs=[pl.BlockSpec(memory_space=pltpu.SMEM)] * 4
        + [pl.BlockSpec(memory_space=pl.ANY)] * (len(pieces) + len(weights))
        + [vmem] * 2,
        out_specs=[vmem] * 5,
        out_shape=[
            jax.ShapeDtypeStruct((kv_width, blocks // 2 * block), jnp.bfloat16),
            jax.ShapeDtypeStruct((blocks // 2, width - kv_width, block), jnp.bfloat16),
            jax.ShapeDtypeStruct((kv_width, WINDOW_KEYS), jnp.bfloat16),
            *[jax.ShapeDtypeStruct((blocks // 4, width - kv_width, block), jnp.bfloat16)] * 2,
        ],
        scratch_shapes=[
            pltpu.VMEM((blocks // 2, features, 2 * block), jnp.bfloat16),
            pltpu.VMEM((features, width), jnp.bfloat16),
            pltpu.VMEM((kv_width, blocks * block), jnp.bfloat16),
            pltpu.VMEM((blocks, width - kv_width, block), jnp.bfloat16),
            pltpu.VMEM((blocks // 2 * block + WINDOW_KEYS, HEAD_WIDTH), jnp.bfloat16),
            pltpu.VMEM((HEAD_WIDTH, blocks // 2 * block + WINDOW_KEYS), jnp.bfloat16),
            pltpu.SemaphoreType.DMA((len(pieces) + len(weights),)),
        ],
        compiler_params=pltpu.CompilerParams(vmem_limit_bytes=wide_vmem_bytes),
        cost_estimate=small_cost,
        name="project",
    )(zs, order, first, sinks, *pieces, *weights, cosine, sine)


def first_part(weights):
    rows = weights[0].shape[0]
    return rows if len(weights) > 1 else rows // 32 * 16 + 16


def sums_kernel(sides, *refs, count, crossing):
    weights, (near0, near1, far0, far1), outs = refs[: 2 * count], refs[2 * count : 2 * count + 4], refs[2 * count + 4 :]
    row, side = sides[0], sides[1]
    middle = outs[0].shape[0]

    def all_of(mine, other):
        start = 0
        for w_near, w_far in zip(weights[:count], weights[count:]):

            def write(halves, place, top, bottom, w_near=w_near, w_far=w_far, start=start):
                near, far = halves
                total = jnp.dot(w_near[...], near[place], preferred_element_type=jnp.float32)
                total += jnp.dot(w_far[...], far[place], preferred_element_type=jnp.float32)
                if count > 1:
                    out = bottom if start else top
                    out[...] = total.astype(out.dtype)
                else:
                    top[...] = total[:middle].astype(top.dtype)
                    bottom[...] = total[middle:].astype(bottom.dtype)

            if crossing:
                write(other, 1 - side, *outs)
            else:
                write(mine, 1 - side, *outs[2:4])
                write(other, side, *outs[4:6])
                write(mine, side, *outs[:2])
            start += w_near.shape[0]

    @pl.when(row == 0)
    def _():
        all_of((near0, far0), (near1, far1))

    @pl.when(row == 1)
    def _():
        all_of((near1, far1), (near0, far0))


def output_sums(sides, w_near, w_far, near, far, crossing):
    depth = sum(w.shape[0] for w in w_near)
    middle = first_part(w_near)
    block = near[0].shape[2]
    vmem = pl.BlockSpec(memory_space=pltpu.VMEM)
    types = [jnp.bfloat16] * 2
    if not crossing:
        types = [jnp.float32, jnp.float32, jnp.bfloat16, jnp.float32, jnp.float32, jnp.bfloat16]
    return pl.pallas_call(
        functools.partial(sums_kernel, count=len(w_near), crossing=crossing),
        in_specs=[pl.BlockSpec(memory_space=pltpu.SMEM)] + [vmem] * (2 * len(w_near) + 4),
        out_specs=[vmem] * len(types),
        out_shape=[
            jax.ShapeDtypeStruct((depth - middle if i % 2 else middle, block), kind) for i, kind in enumerate(types)
        ],
        compiler_params=pltpu.CompilerParams(vmem_limit_bytes=vmem_bytes),
        cost_estimate=small_cost,
        name="crossing_sums" if crossing else "output_sums",
    )(sides, *w_near, *w_far, *near, *far)


def slab_body(tokens, w_query, w_kv, w_out, sinks):
    devices = lax.axis_size("seq")
    slabs = devices // SLICES
    tp = lax.axis_size("tp")
    place = lax.axis_index("seq")
    slab, part = place // SLICES, place % SLICES
    side = lax.axis_index("tp")
    block = tokens.shape[0]
    blocks = SLICES * tp
    both = ("seq", "tp")

    def swap(value, flip_seq, flip_tp):
        pairs = [
            (s * tp + t, (s ^ flip_seq) * tp + (t ^ flip_tp)) for s in range(devices) for t in range(tp)
        ]
        return lax.ppermute(value, both, pairs)

    def turn(value):
        pairs = [(s, (s + SLICES) % devices) for s in range(devices)]
        return lax.ppermute(value, "seq", pairs)

    tie = lambda *values: lax.optimization_barrier(values)

    core, row = part % 2, part // 2
    def of_head(weight, head):
        width = weight.shape[1] // SLICES
        return lax.dynamic_slice_in_dim(weight, head * width, width, 1)

    def by(flag, one, other):
        joined = jnp.concatenate([one, other], axis=0)
        return jnp.where(flag == 1, jnp.concatenate([other, one], axis=0), joined)

    def of_chip(make):
        return by(core, make(part), swap(make(part ^ 1), 1, 0))

    def of_next_chip(make):
        return [swap(make(part ^ 2), 2, 0), swap(make(part ^ 3), 3, 0)]

    def in_head(head):
        return jnp.concatenate([of_head(w_kv, head), of_head(w_query, head)], axis=1)

    def out_head(head):
        return of_head(w_out, head)

    order = jnp.stack(
        [
            (row ^ r) * 2 * tp + (core ^ c) * tp + (side ^ t)
            for r in range(2)
            for c in range(2)
            for t in range(tp)
        ]
    ).astype(jnp.int32)

    own = tokens.T
    features = own.shape[0]
    third = features // 3
    near, far = of_chip(in_head), of_next_chip(in_head)
    near, own_late = tie(near, own)
    a, b, c = (own_late[i * third : (i + 1) * third] for i in range(3))
    next_near = turn(near)
    *far, x_a = tie(*far, swap(a, 0, 1))
    far = by(core, *far)
    weights_in = [by(row, near, far)]
    near, far, x_a, a, b, c = tie(next_near, far, x_a, a, b, c)
    far, x_b, y_b, near, x_a, a, c = tie(turn(far), swap(b, 0, 1), swap(b, 2, 0), near, x_a, a, c)
    weights_in.append(by(row, near, far))
    weight = turn(weights_in[1])
    first = slab * (blocks * block)
    places = first + jnp.arange(blocks * block, dtype=jnp.int32)
    angles = angles_of(places)
    cosine, sine = jnp.cos(angles), jnp.sin(angles)
    slabs_held = jnp.stack([(slab - k) % slabs for k in range(slabs)]).astype(jnp.int32)
    sides = jnp.stack([row, side])
    first_row = jnp.stack([first, core])
    heads = sinks.shape[0] // SLICES
    head_sinks = lax.dynamic_slice_in_dim(sinks, part * heads, heads, 0)
    small = [cosine, sine, slabs_held, order, sides, first_row, head_sinks]
    x_c, y_c, x_a, y_b, a, weights_in[0], *small = tie(
        swap(c, 0, 1), swap(c, 2, 0), x_a, y_b, a, weights_in[0], *small
    )
    cosine, sine, slabs_held, order, sides, first_row, head_sinks = small
    weight, y_a, d_b, x_a, y_c = tie(weight, swap(a, 2, 0), swap(y_b, 0, 1), x_a, y_c)
    cut = weight.shape[0] // 32 * 16 + 16
    weights_in += [weight, turn(weight[:cut]), weight[cut:]]
    d_a, d_c, w_out, *weights_in[-2:] = tie(swap(x_a, 2, 0), swap(y_c, 0, 1), w_out, *weights_in[-2:])
    weights_in[-1] = turn(weights_in[-1])

    def of_cores(*pieces):
        return [*pieces, *(swap(piece, 1, 0) for piece in pieces)]

    pieces = of_cores(own, x_a, x_b, x_c) + of_cores(y_a, y_b, y_c, d_a, d_b, d_c)
    near_out = of_chip(out_head)
    far_out = of_next_chip(out_head)
    *pieces, far_out[0], far_out[1] = tie(*pieces, *far_out)
    own_out = by(row, near_out, by(core, *far_out))
    own_out_late, weights_in[-1] = tie(own_out, weights_in[-1])
    weights_out = [own_out, turn(own_out_late)]
    kv, q, kv_tail, *later = project(slabs_held, order, first_row, head_sinks, pieces, weights_in, cosine, sine)
    kv_tail = shift(kv_tail, "seq", SLICES)
    kv_tail, weights_out[1] = tie(kv_tail, weights_out[1])
    mixed = [None, later]
    mixed[0] = attend(first_row, head_sinks, q, kv, 0, (kv_tail,))
    came = [swap(give, 1, 0) for give, _ in mixed]
    kept = [keep for _, keep in mixed]

    depth = weights_out[0].shape[0]
    result = jnp.zeros((features, block), jnp.bfloat16)
    weights_out.append(turn(weights_out[1]))
    chunks = ((0, 1), (2,), (3,))
    sums, plain, merged = [], [], []
    for n, chunk in enumerate(chunks):
        w_near = [weights_out[k] for k in chunk]
        w_far = [swap(w, 1, 0) for w in w_near]
        crosses = output_sums(sides, w_near, w_far, kept, came, True)
        by_x, by_y = swap(crosses[0], 0, 1), swap(crosses[1], 2, 0)
        *own_sums, x_top, x_bottom, y_top, y_bottom = output_sums(sides, w_near, w_far, kept, came, False)
        if n == 0:
            own_sums[0], weights_out[2] = tie(own_sums[0], weights_out[2])
            weights_out.append(turn(weights_out[2]))
        plain.append([swap(x_top, 0, 1), swap(y_bottom, 2, 0)])
        if n:
            by_x, by_y, *merged[n - 1] = tie(by_x, by_y, *merged[n - 1])
        else:
            by_x, by_y = tie(by_x, by_y)
        y_top = (y_top + by_x.astype(jnp.float32)).astype(jnp.bfloat16)
        x_bottom = (x_bottom + by_y.astype(jnp.float32)).astype(jnp.bfloat16)
        if n + 1 < len(chunks):
            kept[0], *plain[n] = tie(kept[0], *plain[n])
        merged.append([swap(x_bottom, 0, 1), swap(y_top, 2, 0)])
        sums.append(own_sums)
    for n, chunk in enumerate(chunks):
        top = sums[n][0] + plain[n][0].astype(jnp.float32) + merged[n][1].astype(jnp.float32)
        bottom = sums[n][1] + merged[n][0].astype(jnp.float32) + plain[n][1].astype(jnp.float32)
        place = (slab - chunk[0]) % slabs * depth
        result = lax.dynamic_update_slice_in_dim(result, top.astype(jnp.bfloat16), place, 0)
        place = (slab - chunk[1]) % slabs * depth if len(chunk) > 1 else place + top.shape[0]
        result = lax.dynamic_update_slice_in_dim(result, bottom.astype(jnp.bfloat16), place, 0)
    return result.T


def rotary(vectors, places):
    half_dim = vectors.shape[-1] // 2
    angles = angles_of(places).T[:, None, :]
    cosine = jnp.cos(angles)
    sine = jnp.sin(angles)
    lower_half = vectors[..., :half_dim]
    upper_half = vectors[..., half_dim:]
    return jnp.concatenate(
        [lower_half * cosine - upper_half * sine, upper_half * cosine + lower_half * sine], axis=-1
    )


def attend_rows(query_rows, key_value_rows, sink_scores, query_pos, key_pos):
    key_part = key_value_rows[:, :, 0, :]
    value_part = key_value_rows[:, :, 1, :]
    scores = jnp.einsum(
        "qhgd,khd->hgqk", query_rows, key_part, preferred_element_type=jnp.float32
    ) * HEAD_WIDTH ** (-0.5)
    allowed = (
        (key_pos[None, :] <= query_pos[:, None])
        & (key_pos[None, :] > query_pos[:, None] - WINDOW_KEYS)
        & (key_pos[None, :] >= 0)
    )
    scores = jnp.where(allowed[None, None], scores, -jnp.inf)
    row_max = jnp.maximum(jnp.max(scores, axis=-1), sink_scores[:, :, None])
    exponent = jnp.exp(scores - row_max[..., None])
    denominator = jnp.sum(exponent, axis=-1) + jnp.exp(sink_scores[:, :, None] - row_max)
    weights = exponent.astype(jnp.bfloat16)
    mixture = jnp.einsum("hgqk,khd->qhgd", weights, value_part, preferred_element_type=jnp.float32)
    return (mixture / jnp.transpose(denominator, (2, 0, 1))[..., None]).astype(jnp.bfloat16)


def finish(kv_sum, places, kv_heads):
    split_key_value = kv_sum.reshape(kv_sum.shape[0], kv_heads, 2, HEAD_WIDTH)
    key_part = rotary(split_key_value[:, :, 0, :], places)
    return jnp.stack([key_part, split_key_value[:, :, 1, :]], axis=2).astype(jnp.bfloat16)


def row_body(tokens, w_query, w_kv, w_out, sinks):
    token_rows = lax.all_gather(tokens, "tp", axis=0, tiled=True)
    row_count = token_rows.shape[0]
    kv_width = w_kv.shape[1]
    kv_heads = kv_width // (2 * HEAD_WIDTH)
    q_width = w_query.shape[1]
    head_groups = q_width // HEAD_WIDTH // kv_heads
    start_pos = lax.axis_index("seq") * row_count
    query_pos = start_pos + jnp.arange(row_count, dtype=jnp.int32)
    key_pos = start_pos - WINDOW_KEYS + jnp.arange(row_count + WINDOW_KEYS, dtype=jnp.int32)
    query_sum = jnp.dot(
        token_rows,
        lax.all_gather(w_query, "seq", axis=0, tiled=True),
        preferred_element_type=jnp.float32,
    )
    kv_sum = jnp.dot(
        token_rows,
        lax.all_gather(w_kv, "seq", axis=0, tiled=True),
        preferred_element_type=jnp.float32,
    )
    query_rows = rotary(
        query_sum.reshape(row_count, kv_heads * head_groups, HEAD_WIDTH), query_pos
    ).astype(jnp.bfloat16)
    query_rows = query_rows.reshape(row_count, kv_heads, head_groups, HEAD_WIDTH)
    local_kv = finish(kv_sum, query_pos, kv_heads).reshape(row_count, kv_width)
    kv_tail = shift(local_kv[row_count - WINDOW_KEYS :], "seq", 1)
    key_value_rows = jnp.concatenate([kv_tail, local_kv], axis=0).reshape(
        row_count + WINDOW_KEYS, kv_heads, 2, HEAD_WIDTH
    )
    attended = attend_rows(
        query_rows, key_value_rows, sinks.reshape(kv_heads, head_groups), query_pos, key_pos
    ).reshape(row_count, q_width)
    out_terms = lax.dot_general(
        attended,
        lax.all_gather(w_out, "seq", axis=0, tiled=True),
        (((1,), (1,)), ((), ())),
        preferred_element_type=jnp.float32,
    )
    return lax.psum_scatter(out_terms.astype(jnp.bfloat16), "tp", scatter_dimension=0, tiled=True)


def solution(mesh):
    in_specs = (P(("seq", "tp"), None), P("seq", "tp"), P("seq", "tp"), P("seq", "tp"), P("tp"))
    out_specs = P(("seq", "tp"), None)

    def body(tokens, w_query, w_kv, w_out, sinks):
        by_slabs = (
            w_kv.shape[1] == SLICES * 2 * HEAD_WIDTH
            and mesh.shape["tp"] == 2
            and mesh.shape["seq"] == 4 * SLICES
            and tokens.shape[0] % (2 * WINDOW_KEYS) == 0
            and (w_query.shape[0] * SLICES) % 16 == 0
        )
        return (slab_body if by_slabs else row_body)(tokens, w_query, w_kv, w_out, sinks)

    return jax.shard_map(body, mesh=mesh, in_specs=in_specs, out_specs=out_specs, check_vma=False)
```
